256 devices in a mesh: row: 32 (over x, y, core), col: 8 (over z).
Axes of the slice: x: 4, y: 4, z: 8, core: 2. Of those that a mesh axis runs over, the one named last changes fastest.
Arguments:
- features: bfloat16 [65536, 256], P(('row', 'col')), may hold values from -6 to 6
- weight_one: bfloat16 [256, 256], replicated, may hold values from -0.375 to 0.375
- weight_two: bfloat16 [256, 172], replicated, may hold values from -0.375 to 0.375
- adj_tiles: bfloat16 [32, 8, 128, 128, 128], P('row', 'col'), may hold values from -0.109375 to 0.109375
- tile_rows: int32 [32, 8, 128], P('row', 'col'), may hold values from 0 to 15
- tile_cols: int32 [32, 8, 128], P('row', 'col'), may hold values from 0 to 63
- tile_counts: int32 [32, 8], P('row', 'col'), may hold values from 32 to 128, as said below
- labels: int32 [65536], P('row'), may hold values from 0 to 171
Outputs:
- logits: float32 [65536, 172], P(('row', 'col'))
- grad_one: float32 [256, 256], replicated
- grad_two: float32 [256, 172], replicated
The draws below stay inside these ranges and needn't reach their ends.
Inputs may be any that keep to these rules, and one draw needn't show every extreme that they name: `tile_counts`: one device has all 128 slots live.
All inputs are finite; a program needn't handle non-finite values.
Results may differ from the reference program's by a relative error of at most 0.007.
Values may be sent and summed in bfloat16 or wider, within the bound.
No kernel may reach another device: no remote copies, remote signals or barrier semaphores. Data moves between devices by JAX's collectives and lax.ppermute only.
A program may use at most 64 MiB of HBM per device.

```python
import jax
import jax.numpy as jnp
from jax import lax

F = 256
HID = 256
C = 172
TB = 128
BL = 2
SLOTS = 128
RBLK = 16
CBLK = 64
NODES = 65536
N_ROW = 32
N_COL = 8


def draw_tile_counts(key, part):
    key = jax.random.fold_in(key, 7)
    first_key, second_key = jax.random.split(key)
    counts = jax.random.randint(first_key, (N_ROW * N_COL,), max(1, SLOTS // 4), SLOTS + 1)
    busiest = jax.random.randint(second_key, (), 0, N_ROW * N_COL)
    device_ids = jnp.arange(N_ROW * N_COL)
    counts = jnp.where(device_ids == busiest, SLOTS, counts)
    return counts.reshape(N_ROW, N_COL).astype(jnp.int32)


def plant(result, stream_key, least, top_value):
    longest = result.shape.index(max(result.shape))
    spots = []
    for shift in (0, 1):
        where = [jax.random.randint(jax.random.fold_in(stream_key, axis), (), 0, length) for axis, length in enumerate(result.shape)]
        where[longest] = (where[longest] + shift) % result.shape[longest]
        spots.append(tuple(where))
    return result.at[spots[0]].set(least).at[spots[1]].set(top_value)


def steps_of(stream_key, extent, pieces, least, top_value):
    loudness, own = 1.0, jax.random.fold_in(stream_key, 6)
    for dim, parts in pieces:
        heights = jnp.exp(jax.random.uniform(jax.random.fold_in(own, dim), (parts,), jnp.float32, least / len(pieces), top_value / len(pieces)))
        loudness = loudness * jnp.repeat(heights, extent[dim] // parts).reshape([-1 if axis == dim else 1 for axis in range(len(extent))])
    return loudness


def scatter_about(own_key, shape, scale, reach, cuts=(), kind=jnp.bfloat16):
    drawn = jax.random.normal(own_key, shape, jnp.float32) * scale
    if len(cuts) > 0:
        drawn = steps_of(own_key, shape, cuts, -0.22, 0.18) * drawn
    return jnp.clip(drawn, min=-reach, max=reach).astype(kind)


def setup_inputs(seed: int = 0) -> dict:
    key_list = jax.random.split(jax.random.key(seed), 9)
    features = scatter_about(key_list[0], (NODES, F), 1.0, 6.0, ((0, 256),))
    weight_one = scatter_about(key_list[1], (F, HID), F ** -0.5, 0.375)
    weight_two = scatter_about(key_list[2], (HID, C), HID ** -0.5, 0.375)
    adj_tiles = scatter_about(key_list[3], (N_ROW, N_COL, SLOTS, TB, TB), (TB * SLOTS // (3 * BL)) ** -0.5, 0.109375, ((0, 32), (1, 8)))
    tile_rows = plant(jax.random.randint(key_list[4], (N_ROW, N_COL, SLOTS), 0, RBLK), jax.random.fold_in(key_list[4], 1), 0, RBLK - 1).astype(jnp.int32)
    tile_cols = plant(jax.random.randint(key_list[5], (N_ROW, N_COL, SLOTS), 0, CBLK), jax.random.fold_in(key_list[5], 1), 0, CBLK - 1).astype(jnp.int32)
    tile_counts = draw_tile_counts(jax.random.fold_in(key_list[8], 71), 0)
    labels = plant(jax.random.randint(key_list[7], (NODES,), 0, C), jax.random.fold_in(key_list[7], 1), 0, C - 1).astype(jnp.int32)
    return {"features": features, "weight_one": weight_one, "weight_two": weight_two, "adj_tiles": adj_tiles, "tile_rows": tile_rows, "tile_cols": tile_cols, "tile_counts": tile_counts, "labels": labels}


def spread(tile_block, row_ids, col_ids, tile_count, source, out_blocks, transposed):
    slot_ids = jnp.arange(tile_block.shape[0], dtype=jnp.int32)
    live_mask = slot_ids < tile_count
    wide_tiles = tile_block.astype(jnp.float32)
    if transposed:
        picked = source[row_ids].astype(jnp.float32)
        product = jnp.einsum("sji,sjw->siw", wide_tiles, picked, precision=lax.Precision.HIGHEST)
        target = col_ids
    else:
        picked = source[col_ids].astype(jnp.float32)
        product = jnp.einsum("sij,sjw->siw", wide_tiles, picked, precision=lax.Precision.HIGHEST)
        target = row_ids
    block_ids = jnp.arange(out_blocks, dtype=jnp.int32)
    places = jnp.logical_and(target[:, None] == block_ids[None, :], live_mask[:, None]).astype(jnp.float32)
    return jnp.einsum("sr,siw->riw", places, product, precision=lax.Precision.HIGHEST)


def forward_spread(adj_tiles, tile_rows, tile_cols, tile_counts, source):
    feat_width = source.shape[-1]
    node_grid = source.reshape(N_ROW, N_COL, BL, TB, feat_width)

    def visit(running, device):
        row_pos = device // N_COL
        col_pos = device % N_COL
        col_panel = node_grid[:, col_pos].reshape(N_ROW * BL, TB, feat_width)
        contrib = spread(adj_tiles[row_pos, col_pos], tile_rows[row_pos, col_pos], tile_cols[row_pos, col_pos], tile_counts[row_pos, col_pos], col_panel, N_COL * BL, False)
        return running.at[row_pos].add(contrib), None

    start_value = jnp.zeros((N_ROW, N_COL * BL, TB, feat_width), jnp.float32)
    running, unused = lax.scan(visit, start_value, jnp.arange(N_ROW * N_COL, dtype=jnp.int32))
    return running.reshape(NODES, feat_width)


def backward_spread(adj_tiles, tile_rows, tile_cols, tile_counts, source):
    feat_width = source.shape[-1]
    node_grid = source.reshape(N_ROW, N_COL * BL, TB, feat_width)

    def visit(running, device):
        row_pos = device // N_COL
        col_pos = device % N_COL
        contrib = spread(adj_tiles[row_pos, col_pos], tile_rows[row_pos, col_pos], tile_cols[row_pos, col_pos], tile_counts[row_pos, col_pos], node_grid[row_pos], N_ROW * BL, True)
        return running.at[:, col_pos].add(contrib.reshape(N_ROW, BL, TB, feat_width)), None

    start_value = jnp.zeros((N_ROW, N_COL, BL, TB, feat_width), jnp.float32)
    running, unused = lax.scan(visit, start_value, jnp.arange(N_ROW * N_COL, dtype=jnp.int32))
    return running.reshape(NODES, feat_width)


def reference(features, weight_one, weight_two, adj_tiles, tile_rows, tile_cols, tile_counts, labels):
    aggregated = forward_spread(adj_tiles, tile_rows, tile_cols, tile_counts, features).astype(jnp.bfloat16)
    hidden_pre = jnp.dot(aggregated, weight_one, preferred_element_type=jnp.float32)
    hidden = jax.nn.silu(hidden_pre).astype(jnp.bfloat16)
    projected = jnp.dot(hidden, weight_two, preferred_element_type=jnp.float32).astype(jnp.bfloat16)
    logits = forward_spread(adj_tiles, tile_rows, tile_cols, tile_counts, projected)
    softened = jax.nn.softmax(logits, axis=-1)
    class_ids = jnp.arange(C, dtype=jnp.int32)
    onehot = (labels[:, None] == class_ids[None, :]).astype(jnp.float32)
    out_grad = ((softened - onehot) * (NODES ** -0.5)).astype(jnp.bfloat16)
    back_grad = backward_spread(adj_tiles, tile_rows, tile_cols, tile_counts, out_grad).astype(jnp.bfloat16)
    grad_two = jnp.dot(hidden.T, back_grad, preferred_element_type=jnp.float32)
    hidden_grad = jnp.dot(back_grad, weight_two.T, preferred_element_type=jnp.float32)
    gate_value = jax.nn.sigmoid(hidden_pre)
    derivative = gate_value * (1.0 + hidden_pre * (1.0 - gate_value))
    pre_grad = (hidden_grad * derivative).astype(jnp.bfloat16)
    grad_one = jnp.dot(aggregated.T, pre_grad, preferred_element_type=jnp.float32)
    return logits, grad_one, grad_two
```

```python
import functools

import jax
import jax.numpy as jnp
from jax import lax
from jax.experimental import pallas as pl
from jax.experimental.pallas import tpu as pltpu
from jax.sharding import PartitionSpec as P

F32 = jnp.float32
BF16 = jnp.bfloat16
NT = (((1,), (1,)), ((), ()))
NN = (((1,), (0,)), ((), ()))
TB = 128
GX, GY, GZ = 4, 4, 8
ROWS = 256
FEAT = 256
CLASSES = 172
CPAD = 176
SLOTS = 128
FWD = 4
BWD = 2
FWD_GROUPS = 48
BWD_GROUPS = 98
VMEM_LIMIT = 56 * 1024 * 1024


def params():
    return pltpu.CompilerParams(vmem_limit_bytes=VMEM_LIMIT)


def any_spec():
    return pl.BlockSpec(memory_space=pl.ANY)


def vmem_spec():
    return pl.BlockSpec(memory_space=pltpu.VMEM)


def smem_spec():
    return pl.BlockSpec(memory_space=pltpu.SMEM)


def row_perm(move):
    pairs = []
    for index in range(GX * GY * 2):
        x, y, core = index // (2 * GY), (index // 2) % GY, index % 2
        x, y, core = move(x, y, core)
        pairs.append((index, ((x % GX) * GY + y % GY) * 2 + core))
    return pairs


def first_axis(step):
    return row_perm(lambda x, y, c: (x, y + step, c) if c == 0 else (x + step, y, c))


def second_axis(step):
    return row_perm(lambda x, y, c: (x + step, y, c) if c == 0 else (x, y + step, c))


def swap_core():
    return row_perm(lambda x, y, c: (x, y, 1 - c))


def gather_row(own):
    send = lambda v, perm: lax.ppermute(v, "row", perm)
    line = jnp.concatenate(
        [
            own,
            send(own, first_axis(-1)),
            send(own, first_axis(2)),
            send(own, first_axis(1)),
        ],
        0,
    )
    line_swap = send(line, swap_core())
    half = line.shape[0] // 2
    plus = send(line, second_axis(-1))
    minus = send(line, second_axis(1))
    two_low = send(line[:half], second_axis(2))
    two_high = send(plus[half:], second_axis(-1))
    two = jnp.concatenate([two_low, two_high], 0)
    return [
        line,
        plus,
        two,
        minus,
        line_swap,
        send(plus, swap_core()),
        send(two, swap_core()),
        send(minus, swap_core()),
    ]


def source_slots(col_ids):
    me = lax.axis_index("row")
    x, y, core = me // (2 * GY), (me // 2) % GY, me % 2
    device = col_ids // 2
    dx = (device // (2 * GY) - x) % GX
    dy = ((device // 2) % GY - y) % GY
    other = device % 2
    along_first = jnp.where(other == 0, dy, dx)
    along_second = jnp.where(other == 0, dx, dy)
    far = (other != core).astype(jnp.int32)
    return ((far * 4 + along_second) * 4 + along_first) * 2 + col_ids % 2


def gather_col(own):
    send = lambda v, step: lax.ppermute(v, "col", [(i, (i + step) % GZ) for i in range(GZ)])
    found = {0: own}
    up = down = own
    for step in range(1, 4):
        up, down = send(up, -1), send(down, 1)
        found[step], found[GZ - step] = up, down
    found[4] = send(up, -1)
    return [found[d] for d in range(GZ)]


def group_tiles(target, source, count, n_targets, group, n_groups):
    slots = jnp.arange(SLOTS, dtype=jnp.int32)
    live = slots < count
    key = jnp.where(live, target, n_targets)
    targets = jnp.arange(n_targets, dtype=jnp.int32)
    members = jnp.sum((key[None, :] == targets[:, None]).astype(jnp.int32), 1)
    groups = (members + group - 1) // group
    earlier = jnp.sum(
        jnp.where(targets[None, :] < key[:, None], groups[None, :], 0), 1
    )
    rank = jnp.sum(
        ((key[None, :] == key[:, None]) & (slots[None, :] < slots[:, None])).astype(jnp.int32), 1
    )
    place = jnp.where(live, earlier * group + rank, -1)
    places = jnp.arange(n_groups * group, dtype=jnp.int32)
    hit = place[None, :] == places[:, None]
    order = SLOTS + jnp.sum(jnp.where(hit, slots[None, :] - SLOTS, 0), 1)
    picked = jnp.sum(jnp.where(hit, source[None, :], 0), 1)
    goal = jnp.sum(jnp.where(hit, target[None, :], 0), 1)[::group]
    return jnp.concatenate([order, picked, goal, jnp.sum(groups)[None]]).astype(jnp.int32)


def load_tiles(tiles_hbm, tiles, sem):
    copy = pltpu.make_async_copy(tiles_hbm, tiles.at[pl.ds(0, SLOTS)], sem)
    copy.start()
    tiles[SLOTS] = jnp.zeros((TB, TB), BF16)
    return copy


def aggregate_kernel(table, tiles_hbm, *rest):
    pieces, (out, tiles, source, total, sems) = rest[:8], rest[8:]
    copies = [load_tiles(tiles_hbm, tiles, sems.at[0])]
    for index, piece in enumerate(pieces):
        copy = pltpu.make_async_copy(piece, source.at[pl.ds(index * 8, 8)], sems.at[index + 1])
        copy.start()
        copies.append(copy)
    total[...] = jnp.zeros_like(total)
    for copy in copies:
        copy.wait()
    width = FWD_GROUPS * FWD

    def product(g):
        left, right = [], []
        for k in range(FWD):
            left.append(tiles[table[g * FWD + k]])
            right.append(source[table[width + g * FWD + k]])
        return lax.dot_general(
            jnp.concatenate(left, 1),
            jnp.concatenate(right, 0),
            NN,
            preferred_element_type=F32,
        )

    def step(i, carry):
        first, second = product(2 * i), product(2 * i + 1)
        total[table[2 * width + 2 * i]] += first
        total[table[2 * width + 2 * i + 1]] += second
        return carry

    lax.fori_loop(0, (table[2 * width + FWD_GROUPS] + 1) // 2, step, 0)
    for d in range(GZ):
        out[d, 0:TB] = total[2 * d].astype(BF16)
        out[d, TB : 2 * TB] = total[2 * d + 1].astype(BF16)


def aggregate(table, tiles, pieces):
    return pl.pallas_call(
        aggregate_kernel,
        name="aggregate",
        out_shape=jax.ShapeDtypeStruct((GZ, ROWS, FEAT), BF16),
        in_specs=[smem_spec()] + [any_spec()] * 9,
        out_specs=vmem_spec(),
        scratch_shapes=[
            pltpu.VMEM((SLOTS + 1, TB, TB), BF16),
            pltpu.VMEM((64, TB, FEAT), BF16),
            pltpu.VMEM((16, TB, FEAT), F32),
            pltpu.SemaphoreType.DMA((9,)),
        ],
        compiler_params=params(),
        cost_estimate=pl.CostEstimate(flops=2 * 10**9, bytes_accessed=10**7, transcendentals=0),
    )(table, tiles, *[p.reshape(8, TB, FEAT) for p in pieces])


def middle_kernel(parts, weight_one, weight_two_t, agg, projected_t):
    summed = parts[0].astype(F32)
    for d in range(1, GZ):
        summed += parts[d].astype(F32)
    rounded = summed.astype(BF16)
    agg[...] = rounded
    pre = lax.dot_general(rounded, weight_one[...], NN, preferred_element_type=F32)
    hidden = (pre * jax.nn.sigmoid(pre)).astype(BF16)
    projected_t[...] = lax.dot_general(
        weight_two_t[...], hidden, NT, preferred_element_type=F32
    ).astype(BF16)


def middle(parts, weight_one, weight_two_t):
    return pl.pallas_call(
        middle_kernel,
        name="middle",
        out_shape=(
            jax.ShapeDtypeStruct((ROWS, FEAT), BF16),
            jax.ShapeDtypeStruct((CPAD, ROWS), BF16),
        ),
        in_specs=[vmem_spec()] * 3,
        out_specs=[vmem_spec()] * 2,
        compiler_params=params(),
    )(parts, weight_one, weight_two_t)


def logits_kernel(table, tiles_hbm, *rest):
    pieces, (out, tiles, source, total, sems) = rest[:8], rest[8:]
    copies = [load_tiles(tiles_hbm, tiles, sems.at[0])]
    for index, piece in enumerate(pieces):
        for block in range(4):
            for half in range(2):
                copy = pltpu.make_async_copy(
                    piece.at[block, :, pl.ds(half * TB, TB)],
                    source.at[(index * 4 + block) * 2 + half],
                    sems.at[index + 1],
                )
                copy.start()
                copies.append(copy)
    total[...] = jnp.zeros_like(total)
    for copy in copies:
        copy.wait()
    width = FWD_GROUPS * FWD

    def product(g):
        left, right = [], []
        for k in range(FWD):
            left.append(source[table[width + g * FWD + k]])
            right.append(tiles[table[g * FWD + k]])
        return lax.dot_general(
            jnp.concatenate(left, 1),
            jnp.concatenate(right, 1),
            NT,
            preferred_element_type=F32,
        )

    def step(i, carry):
        first, second = product(2 * i), product(2 * i + 1)
        total[table[2 * width + 2 * i]] += first
        total[table[2 * width + 2 * i + 1]] += second
        return carry

    lax.fori_loop(0, (table[2 * width + FWD_GROUPS] + 1) // 2, step, 0)
    for d in range(GZ):
        out[d, :, 0:TB] = total[2 * d].astype(BF16)
        out[d, :, TB : 2 * TB] = total[2 * d + 1].astype(BF16)


def partial_logits(table, tiles, pieces):
    return pl.pallas_call(
        logits_kernel,
        name="partial_logits",
        out_shape=jax.ShapeDtypeStruct((GZ, CPAD, ROWS), BF16),
        in_specs=[smem_spec()] + [any_spec()] * 9,
        out_specs=vmem_spec(),
        scratch_shapes=[
            pltpu.VMEM((SLOTS + 1, TB, TB), BF16),
            pltpu.VMEM((64, CPAD, TB), BF16),
            pltpu.VMEM((16, CPAD, TB), F32),
            pltpu.SemaphoreType.DMA((9,)),
        ],
        compiler_params=params(),
        cost_estimate=pl.CostEstimate(flops=2 * 10**9, bytes_accessed=10**7, transcendentals=0),
    )(table, tiles, *[p.reshape(4, CPAD, ROWS) for p in pieces])


def loss_kernel(scale, parts, labels, logits, grad_t):
    summed = parts[0].astype(F32)
    for d in range(1, GZ):
        summed += parts[d].astype(F32)
    logits[...] = jnp.transpose(summed)[:, :CLASSES]
    ids = lax.broadcasted_iota(jnp.int32, summed.shape, 0)
    valid = ids < CLASSES
    top = jnp.max(jnp.where(valid, summed, -jnp.inf), 0, keepdims=True)
    grown = jnp.where(valid, jnp.exp(summed - top), 0.0)
    soft = grown / jnp.sum(grown, 0, keepdims=True)
    onehot = (ids == labels[...]).astype(F32)
    grad_t[...] = ((soft - onehot) * scale).astype(BF16)


def loss_grad(parts, labels, scale):
    return pl.pallas_call(
        functools.partial(loss_kernel, scale),
        name="loss_grad",
        out_shape=(
            jax.ShapeDtypeStruct((ROWS, CLASSES), F32),
            jax.ShapeDtypeStruct((CPAD, ROWS), BF16),
        ),
        in_specs=[vmem_spec()] * 2,
        out_specs=[vmem_spec()] * 2,
        compiler_params=params(),
    )(parts, labels)


def gates_kernel(agg, weight_one_t, hidden_t, slope_t):
    pre = lax.dot_general(weight_one_t[...], agg[...], NT, preferred_element_type=F32)
    gate = jax.nn.sigmoid(pre)
    hidden_t[...] = (pre * gate).astype(BF16)
    slope_t[...] = (gate * (1.0 + pre * (1.0 - gate))).astype(BF16)


def gates(agg_panel, weight_one_t):
    nodes = agg_panel.shape[0]
    chunk = 1024
    return pl.pallas_call(
        gates_kernel,
        name="gates",
        grid=(nodes // chunk,),
        out_shape=(
            jax.ShapeDtypeStruct((FEAT, nodes), BF16),
            jax.ShapeDtypeStruct((FEAT, nodes), BF16),
        ),
        in_specs=[
            pl.BlockSpec((chunk, FEAT), lambda i: (i, 0)),
            pl.BlockSpec((FEAT, FEAT), lambda i: (0, 0)),
        ],
        out_specs=[
            pl.BlockSpec((FEAT, chunk), lambda i: (0, i)),
            pl.BlockSpec((FEAT, chunk), lambda i: (0, i)),
        ],
        compiler_params=params(),
        cost_estimate=pl.CostEstimate(
            flops=2 * nodes * FEAT * FEAT, bytes_accessed=12 * 10**6, transcendentals=nodes * FEAT
        ),
    )(agg_panel, weight_one_t)


def backward_kernel(
    table, tiles_hbm, hidden_hbm, slope_hbm, agg_hbm, weight_two, *rest
):
    pieces, rest = rest[:GZ], rest[GZ:]
    out, tiles, grads, total, hidden, slope, agg, sum_one, sum_two, sems = rest
    copies = [load_tiles(tiles_hbm, tiles, sems.at[0])]
    for d, piece in enumerate(pieces):
        for half in range(2):
            copy = pltpu.make_async_copy(
                piece.at[:, pl.ds(half * TB, TB)], grads.at[2 * d + half], sems.at[1]
            )
            copy.start()
            copies.append(copy)
    later = []
    for index, (held, place) in enumerate(((hidden_hbm, hidden), (slope_hbm, slope), (agg_hbm, agg))):
        copy = pltpu.make_async_copy(held, place, sems.at[index + 2])
        copy.start()
        later.append(copy)
    total[...] = jnp.zeros_like(total)
    for copy in copies:
        copy.wait()
    width = BWD_GROUPS * BWD

    def product(g):
        left, right = [], []
        for k in range(BWD):
            left.append(grads[table[width + g * BWD + k]])
            right.append(tiles[table[g * BWD + k]])
        return lax.dot_general(
            jnp.concatenate(left, 1),
            jnp.concatenate(right, 0),
            NN,
            preferred_element_type=F32,
        )

    def step(i, carry):
        first, second = product(2 * i), product(2 * i + 1)
        total[table[2 * width + 2 * i]] += first
        total[table[2 * width + 2 * i + 1]] += second
        return carry

    lax.fori_loop(0, (table[2 * width + BWD_GROUPS] + 1) // 2, step, 0)
    sum_one[...] = jnp.zeros_like(sum_one)
    sum_two[...] = jnp.zeros_like(sum_two)
    for copy in later:
        copy.wait()
    blocks = 8
    span = blocks * TB

    def finish(i, carry):
        back = jnp.concatenate([total[i * blocks + k] for k in range(blocks)], 1).astype(BF16)
        start = pl.multiple_of(i * span, span)
        grad = lax.dot_general(weight_two[...], back, NN, preferred_element_type=F32)
        grad = (grad * slope[:, pl.ds(start, span)].astype(F32)).astype(BF16)
        sum_one[...] += lax.dot_general(
            grad, agg[pl.ds(start, span), :], NN, preferred_element_type=F32
        )
        sum_two[...] += lax.dot_general(
            back, hidden[:, pl.ds(start, span)], NT, preferred_element_type=F32
        )
        return carry

    lax.fori_loop(0, 64 // blocks, finish, 0)
    out[0:FEAT] = sum_one[...].astype(BF16)
    out[FEAT : FEAT + CPAD] = sum_two[...].astype(BF16)
    out[FEAT + CPAD :] = jnp.zeros((512 - FEAT - CPAD, FEAT), BF16)


def backward(table, tiles, hidden_t, slope_t, agg_panel, weight_two, pieces):
    nodes = agg_panel.shape[0]
    return pl.pallas_call(
        backward_kernel,
        name="backward",
        out_shape=jax.ShapeDtypeStruct((512, FEAT), BF16),
        in_specs=[smem_spec()] + [any_spec()] * 4 + [vmem_spec()] + [any_spec()] * GZ,
        out_specs=vmem_spec(),
        scratch_shapes=[
            pltpu.VMEM((SLOTS + 1, TB, TB), BF16),
            pltpu.VMEM((16, CPAD, TB), BF16),
            pltpu.VMEM((64, CPAD, TB), F32),
            pltpu.VMEM((FEAT, nodes), BF16),
            pltpu.VMEM((FEAT, nodes), BF16),
            pltpu.VMEM((nodes, FEAT), BF16),
            pltpu.VMEM((FEAT, FEAT), F32),
            pltpu.VMEM((CPAD, FEAT), F32),
            pltpu.SemaphoreType.DMA((5,)),
        ],
        compiler_params=params(),
        cost_estimate=pl.CostEstimate(flops=5 * 10**9, bytes_accessed=2 * 10**7, transcendentals=0),
    )(table, tiles, hidden_t, slope_t, agg_panel, weight_two, *pieces)


def sum_everywhere(grads):
    shares = lax.all_to_all(grads.reshape(32, 16, FEAT), "row", 0, 0, tiled=True)
    share = jnp.sum(shares.astype(F32), 0).astype(BF16)
    shares = lax.all_to_all(
        jnp.broadcast_to(share, (GZ, 16, FEAT)), "col", 0, 0, tiled=True
    )
    share = jnp.sum(shares.astype(F32), 0).astype(BF16)
    full = lax.all_to_all(jnp.broadcast_to(share, (32, 16, FEAT)), "row", 0, 0, tiled=True)
    return full.reshape(512, FEAT)


def body(features, weight_one, weight_two, adj_tiles, tile_rows, tile_cols, tile_counts, labels):
    tiles = adj_tiles[0, 0]
    row_ids = tile_rows[0, 0]
    col_ids = tile_cols[0, 0]
    count = tile_counts[0, 0]
    z = lax.axis_index("col")
    node_total = ROWS * lax.axis_size("row") * lax.axis_size("col")
    weight_one_t = weight_one.T
    weight_two_pad = jnp.pad(weight_two, ((0, 0), (0, CPAD - CLASSES)))
    weight_two_t = weight_two_pad.T
    own_labels = lax.dynamic_slice_in_dim(labels, z * ROWS, ROWS, 0)[None, :]
    forward = group_tiles(row_ids, source_slots(col_ids), count, 16, FWD, FWD_GROUPS)
    row_slots = ((row_ids // 2 - z) % GZ) * 2 + row_ids % 2
    reverse = group_tiles(col_ids, row_slots, count, 64, BWD, BWD_GROUPS)

    parts = aggregate(forward, tiles, gather_row(features))
    parts = lax.all_to_all(parts, "col", 0, 0, tiled=True)
    agg, projected_t = middle(parts, weight_one, weight_two_t)
    agg_panel = lax.all_gather(agg, "row", axis=0, tiled=True)
    parts = partial_logits(forward, tiles, gather_row(projected_t))
    parts = lax.all_to_all(parts, "col", 0, 0, tiled=True)
    logits, grad_t = loss_grad(parts, own_labels, node_total ** (-0.5))
    grad_pieces = gather_col(grad_t)
    hidden_t, slope_t = gates(agg_panel, weight_one_t)
    grads = backward(reverse, tiles, hidden_t, slope_t, agg_panel, weight_two_pad, grad_pieces)
    grads = sum_everywhere(grads)
    grad_one = grads[:FEAT].astype(F32).T
    grad_two = grads[FEAT : FEAT + CLASSES].astype(F32).T
    return logits, grad_one, grad_two


def solution(mesh):
    in_specs = (
        P(("row", "col"), None),
        P(),
        P(),
        P("row", "col", None, None, None),
        P("row", "col", None),
        P("row", "col", None),
        P("row", "col"),
        P("row"),
    )
    out_specs = (P(("row", "col"), None), P(), P())
    return jax.shard_map(body, mesh=mesh, in_specs=in_specs, out_specs=out_specs, check_vma=False)
```

```python
import functools

import jax
import jax.numpy as jnp
from jax import lax
from jax.experimental import pallas as pl
from jax.experimental.pallas import tpu as pltpu
from jax.sharding import PartitionSpec as P

F32 = jnp.float32
BF16 = jnp.bfloat16
NT = (((1,), (1,)), ((), ()))
NN = (((1,), (0,)), ((), ()))
TB = 128
GX, GY, GZ = 4, 4, 8
ROWS = 256
FEAT = 256
CLASSES = 172
CPAD = 176
SLOTS = 128
FWD = 4
BWD = 2
UNROLL = 4
FWD_GROUPS = 52
BWD_GROUPS = 100
EARLY = 6
PLACE_OF_OFFSET = (7, 3, 4, 0, 1, 2, 5, 6)


def params(mib):
    return pltpu.CompilerParams(vmem_limit_bytes=mib * 1024 * 1024)


def vmem_spec():
    return pl.BlockSpec(memory_space=pltpu.VMEM)


def hbm_spec():
    return pl.BlockSpec(memory_space=pltpu.HBM)


def smem_spec():
    return pl.BlockSpec(memory_space=pltpu.SMEM)


def hold_kernel(tiles_hbm, after, tiles, sem):
    copy = pltpu.make_async_copy(tiles_hbm, tiles, sem)
    copy.start()
    copy.wait()


def hold_tiles(tiles, after):
    return pl.pallas_call(
        hold_kernel,
        name="hold_tiles",
        out_shape=jax.ShapeDtypeStruct(tiles.shape, tiles.dtype),
        in_specs=[hbm_spec(), vmem_spec()],
        out_specs=vmem_spec(),
        scratch_shapes=[pltpu.SemaphoreType.DMA],
        compiler_params=params(4),
        cost_estimate=pl.CostEstimate(flops=0, bytes_accessed=8 * 10**6, transcendentals=0),
    )(tiles, after)


def row_perm(move):
    pairs = []
    for index in range(GX * GY * 2):
        x, y, core = index // (2 * GY), (index // 2) % GY, index % 2
        x, y, core = move(x, y, core)
        pairs.append((index, ((x % GX) * GY + y % GY) * 2 + core))
    return pairs


def first_axis(step):
    return row_perm(lambda x, y, c: (x, y + step, c) if c == 0 else (x + step, y, c))


def second_axis(step):
    return row_perm(lambda x, y, c: (x + step, y, c) if c == 0 else (x, y + step, c))


def swap_core():
    return row_perm(lambda x, y, c: (x, y, 1 - c))


def gather_row(own, beside=None):
    send = lambda v, perm: lax.ppermute(v, "row", perm)
    line = jnp.concatenate(
        [
            own,
            send(own, first_axis(-1)),
            send(own, first_axis(2)),
            send(own, first_axis(1)),
        ],
        0,
    )
    half = line.shape[0] // 2
    plus = send(line, second_axis(-1))
    minus = send(line, second_axis(1))
    two_low = send(line[:half], second_axis(2))
    two_high = send(plus[half:], second_axis(-1))
    line, plus = lax.optimization_barrier((line, plus))
    held = None
    if beside is not None:
        minus, held = lax.optimization_barrier((minus, beside(plus)))
    mine = [line, plus, two_low, two_high, minus]
    return mine + [send(v, swap_core()) for v in mine], held


def source_slots(col_ids):
    me = lax.axis_index("row")
    x, y, core = me // (2 * GY), (me // 2) % GY, me % 2
    device = col_ids // 2
    dx = (device // (2 * GY) - x) % GX
    dy = ((device // 2) % GY - y) % GY
    other = device % 2
    along_first = jnp.where(other == 0, dy, dx)
    along_second = jnp.where(other == 0, dx, dy)
    far = (other != core).astype(jnp.int32)
    return ((far * 4 + along_second) * 4 + along_first) * 2 + col_ids % 2


def along_col(value, step):
    return lax.ppermute(value, "col", [(i, (i + step) % GZ) for i in range(GZ)])


def gather_col(own):
    found = {0: own}
    for d in (2, 6, 1, 7):
        found[d] = along_col(own, -d if d < 4 else GZ - d)
    up = jnp.concatenate([found[1], found[2][:, :TB]], 1)
    down = jnp.concatenate([found[7], found[6][:, TB:]], 1)
    up, down = along_col(up, -2), along_col(down, 2)
    found[3], found[5] = up[:, :ROWS], down[:, :ROWS]
    found[4] = jnp.concatenate([up[:, ROWS:], down[:, ROWS:]], 1)
    return [found[d] for d in range(GZ)]


def reduce_col(up, down, late):
    up, down = along_col(up, 2), along_col(down, -2)
    one, two, six, seven = late()
    width = one.shape[1]
    half = jnp.zeros((one.shape[0], width // 2), F32)
    extra_up = jnp.concatenate([up[:, width:].astype(F32), half], 1)
    extra_down = jnp.concatenate([half, down[:, width:].astype(F32)], 1)
    return [
        along_col((two + extra_up).astype(BF16), 2),
        along_col((six + extra_down).astype(BF16), -2),
        along_col((one + up[:, :width].astype(F32)).astype(BF16), 1),
        along_col((seven + down[:, :width].astype(F32)).astype(BF16), -1),
    ]


def group_tiles(target, source, empty, count, n_targets, group, n_groups, early):
    slots = jnp.arange(SLOTS, dtype=jnp.int32)
    live = slots < count
    key = jnp.where(live, target, n_targets)
    targets = jnp.arange(n_targets, dtype=jnp.int32)
    members = jnp.sum((key[None, :] == targets[:, None]).astype(jnp.int32), 1)
    groups = (members + group - 1) // group
    n_early = jnp.sum(jnp.where(targets < early, groups, 0))
    n_early = (n_early + UNROLL - 1) // UNROLL * UNROLL
    n_all = n_early + jnp.sum(jnp.where(targets >= early, groups, 0))
    before = (targets[None, :] < key[:, None]) & (
        (targets[None, :] >= early) == (key[:, None] >= early)
    )
    earlier = jnp.sum(jnp.where(before, groups[None, :], 0), 1)
    earlier = earlier + jnp.where(key >= early, n_early, 0)
    rank = jnp.sum(
        ((key[None, :] == key[:, None]) & (slots[None, :] < slots[:, None])).astype(jnp.int32), 1
    )
    place = jnp.where(live, earlier * group + rank, -1)
    places = jnp.arange(n_groups * group, dtype=jnp.int32)
    hit = place[None, :] == places[:, None]
    order = jnp.sum(jnp.where(hit, slots[None, :], 0), 1)
    picked = empty + jnp.sum(jnp.where(hit, source[None, :] - empty, 0), 1)
    first = place[None, :] == group * jnp.arange(n_groups, dtype=jnp.int32)[:, None]
    goal = jnp.sum(jnp.where(first, target[None, :], 0), 1)
    counts = jnp.where(jnp.arange(2) == 0, n_early, n_all)
    return order, picked, goal, counts


def run_groups(table, group, first, last, shift, product, total):
    order, picked, goal, _ = table

    def step(i, carry):
        made = []
        for u in range(UNROLL):
            start = (i * UNROLL + u) * group
            tiles = [order[start + k] for k in range(group)]
            sources = [picked[start + k] for k in range(group)]
            made.append(product(tiles, sources))
        for u in range(UNROLL):
            total[jnp.maximum(goal[i * UNROLL + u] - shift, 0)] += made[u]
        return carry

    lax.fori_loop(first // UNROLL, (last + UNROLL - 1) // UNROLL, step, 0)


def rows_product(tiles, source):
    def product(picked, origins):
        return lax.dot_general(
            jnp.concatenate([tiles[t] for t in picked], 1),
            jnp.concatenate([source[o] for o in origins], 0),
            NN,
            preferred_element_type=F32,
        )

    return product


def columns_product(tiles, source):
    def product(picked, origins):
        return lax.dot_general(
            jnp.concatenate([source[o] for o in origins], 1),
            jnp.concatenate([tiles[t] for t in picked], 1),
            NT,
            preferred_element_type=F32,
        )

    return product


def halves_of_rows(total, place):
    return jnp.concatenate([total[2 * place], total[2 * place + 1]], 0)


def halves_of_columns(total, place):
    return jnp.concatenate([total[2 * place], total[2 * place + 1]], 1)


def early_outputs(total, whole, out_up, out_down):
    far = whole(total, 1)
    width = far.shape[1]
    out_up[:, :width] = whole(total, 0).astype(BF16)
    out_up[:, width:] = far[:, : width // 2].astype(BF16)
    out_down[:, :width] = whole(total, 2).astype(BF16)
    out_down[:, width:] = far[:, width // 2 :].astype(BF16)


def aggregate_early_kernel(*refs):
    table, (tiles, *rest) = refs[:4], refs[4:]
    pieces, (source, out_up, out_down, total) = rest[:-4], rest[-4:]
    filled = 0
    for piece in pieces:
        for block in range(piece.shape[0] // TB):
            source[filled] = piece[block * TB : (block + 1) * TB]
            filled += 1
    source[filled] = jnp.zeros((TB, FEAT), BF16)
    total[...] = jnp.zeros_like(total)
    run_groups(table, FWD, 0, table[3][0], 0, rows_product(tiles, source), total)
    early_outputs(total, halves_of_rows, out_up, out_down)


def aggregate_late_kernel(*refs):
    table, (tiles, source, *rest) = refs[:4], refs[4:]
    outs, total = rest[:5], rest[5]
    total[...] = jnp.zeros_like(total)
    run_groups(table, FWD, table[3][0], table[3][1], EARLY, rows_product(tiles, source), total)
    for place, out in enumerate(outs):
        out[...] = halves_of_rows(total, place)


def sigmoid(value):
    return 0.5 * jnp.tanh(0.5 * value) + 0.5


def logits_early_kernel(*refs):
    table, (tiles, weight_one, weight_two, *rest) = refs[:4], refs[4:]
    weight_one_t = jnp.transpose(weight_one[...].astype(F32)).astype(BF16)
    weight_two_t = jnp.transpose(weight_two[...].astype(F32)).astype(BF16)
    pieces, rest = rest[:-7], rest[-7:]
    source, out_up, out_down, agg, hidden_t, slope_t, total = rest
    filled = 0
    for piece in pieces:
        nodes = piece.shape[0]
        agg[filled : filled + nodes] = piece[...]
        pre = lax.dot_general(weight_one_t, piece[...], NT, preferred_element_type=F32)
        gate = sigmoid(pre)
        hidden = (pre * gate).astype(BF16)
        hidden_t[:, filled : filled + nodes] = hidden
        slope_t[:, filled : filled + nodes] = (gate * (1.0 + pre * (1.0 - gate))).astype(BF16)
        projected = lax.dot_general(
            weight_two_t, hidden, NN, preferred_element_type=F32
        ).astype(BF16)
        for block in range(nodes // TB):
            source[filled // TB + block] = projected[:, block * TB : (block + 1) * TB]
        filled += nodes
    source[filled // TB] = jnp.zeros((CPAD, TB), BF16)
    total[...] = jnp.zeros_like(total)
    run_groups(table, FWD, 0, table[3][0], 0, columns_product(tiles, source), total)
    early_outputs(total, halves_of_columns, out_up, out_down)


def logits_late_kernel(*refs):
    table, (tiles, source, *rest) = refs[:4], refs[4:]
    outs, total = rest[:5], rest[5]
    total[...] = jnp.zeros_like(total)
    run_groups(table, FWD, table[3][0], table[3][1], EARLY, columns_product(tiles, source), total)
    for place, out in enumerate(outs):
        out[...] = halves_of_columns(total, place)


def spread_and_reduce(early_kernel, late_kernel, name, table, operands, kept, block, out):
    cost = pl.CostEstimate(flops=10**9, bytes_accessed=10**7, transcendentals=0)
    wide = jax.ShapeDtypeStruct((out[0], out[1] * 3 // 2), BF16)
    source, up, down, *kept = pl.pallas_call(
        early_kernel,
        name=name + "_early",
        out_shape=(jax.ShapeDtypeStruct((65, *block), BF16), wide, wide, *kept),
        in_specs=[smem_spec()] * 4 + [vmem_spec()] * len(operands),
        out_specs=[vmem_spec()] * (3 + len(kept)),
        scratch_shapes=[pltpu.VMEM((EARLY, *block), F32)],
        compiler_params=params(10),
        cost_estimate=cost,
    )(*table, *operands)
    one, two, six, seven, own = pl.pallas_call(
        late_kernel,
        name=name + "_late",
        out_shape=(jax.ShapeDtypeStruct(out, F32),) * 5,
        in_specs=[smem_spec()] * 4 + [vmem_spec()] * 2,
        out_specs=[vmem_spec()] * 5,
        scratch_shapes=[pltpu.VMEM((16 - EARLY, *block), F32)],
        compiler_params=params(8),
        cost_estimate=cost,
    )(*table, operands[0], source)
    return [own] + reduce_col(up, down, lambda: (one, two, six, seven)), kept


def add_up(parts):
    summed = parts[0][...].astype(F32)
    for part in parts[1:]:
        summed += part[...].astype(F32)
    return summed


def middle_kernel(*refs):
    parts, agg = refs[:5], refs[5]
    agg[...] = add_up(parts).astype(BF16)


def middle(parts):
    return pl.pallas_call(
        middle_kernel,
        name="middle",
        out_shape=jax.ShapeDtypeStruct((ROWS, FEAT), BF16),
        in_specs=[vmem_spec()] * 5,
        out_specs=vmem_spec(),
        compiler_params=params(8),
    )(*parts)


def loss_kernel(scale, *refs):
    parts, (labels, place, logits, grad_t) = refs[:5], refs[5:]
    summed = add_up(parts)
    logits[...] = jnp.transpose(summed)[:, :CLASSES]
    ids = lax.broadcasted_iota(jnp.int32, summed.shape, 0)
    valid = ids < CLASSES
    top = jnp.max(jnp.where(valid, summed, -jnp.inf), 0, keepdims=True)
    grown = jnp.where(valid, jnp.exp(summed - top), 0.0)
    soft = grown / jnp.sum(grown, 0, keepdims=True)
    onehot = (ids == labels[pl.ds(place[0], 1), :]).astype(F32)
    grad_t[...] = ((soft - onehot) * scale).astype(BF16)


def loss_grad(parts, labels, place, scale):
    return pl.pallas_call(
        functools.partial(loss_kernel, scale),
        name="loss_grad",
        out_shape=(
            jax.ShapeDtypeStruct((ROWS, CLASSES), F32),
            jax.ShapeDtypeStruct((CPAD, ROWS), BF16),
        ),
        in_specs=[vmem_spec()] * 6 + [smem_spec()],
        out_specs=[vmem_spec()] * 2,
        compiler_params=params(8),
    )(*parts, labels, place)


def backward_kernel(*refs):
    table, (tiles, hidden, slope, agg, weight_two, *rest) = refs[:4], refs[4:]
    pieces, (out, grads, total, sum_one, sum_two) = rest[:GZ], rest[GZ:]
    for d, piece in enumerate(pieces):
        grads[2 * d] = piece[:, :TB]
        grads[2 * d + 1] = piece[:, TB:]
    grads[16] = jnp.zeros((CPAD, TB), BF16)
    total[...] = jnp.zeros_like(total)

    def product(picked, origins):
        return lax.dot_general(
            jnp.concatenate([grads[o] for o in origins], 1),
            jnp.concatenate([tiles[t] for t in picked], 0),
            NN,
            preferred_element_type=F32,
        )

    run_groups(table, BWD, 0, table[3][1], 0, product, total)
    sum_one[...] = jnp.zeros_like(sum_one)
    sum_two[...] = jnp.zeros_like(sum_two)
    blocks = 8
    span = blocks * TB

    def finish(i, carry):
        back = jnp.concatenate([total[i * blocks + k] for k in range(blocks)], 1).astype(BF16)
        start = pl.multiple_of(i * span, span)
        grad = lax.dot_general(weight_two[...], back, NN, preferred_element_type=F32)
        grad = (grad * slope[:, pl.ds(start, span)].astype(F32)).astype(BF16)
        sum_one[...] += lax.dot_general(
            grad, agg[pl.ds(start, span), :], NN, preferred_element_type=F32
        )
        sum_two[...] += lax.dot_general(
            back, hidden[:, pl.ds(start, span)], NT, preferred_element_type=F32
        )
        return carry

    lax.fori_loop(0, 64 // blocks, finish, 0)
    out[0:FEAT] = jnp.transpose(sum_one[...]).astype(BF16)
    out[FEAT:, :CPAD] = jnp.transpose(sum_two[...]).astype(BF16)
    out[FEAT:, CPAD:] = jnp.zeros((FEAT, FEAT - CPAD), BF16)


def backward(table, tiles, hidden_t, slope_t, agg_panel, weight_two, pieces):
    return pl.pallas_call(
        backward_kernel,
        name="backward",
        out_shape=jax.ShapeDtypeStruct((512, FEAT), BF16),
        in_specs=[smem_spec()] * 4 + [vmem_spec()] * (5 + GZ),
        out_specs=vmem_spec(),
        scratch_shapes=[
            pltpu.VMEM((17, CPAD, TB), BF16),
            pltpu.VMEM((64, CPAD, TB), F32),
            pltpu.VMEM((FEAT, FEAT), F32),
            pltpu.VMEM((CPAD, FEAT), F32),
        ],
        compiler_params=params(12),
        cost_estimate=pl.CostEstimate(flops=5 * 10**9, bytes_accessed=2 * 10**7, transcendentals=0),
    )(*table, tiles, hidden_t, slope_t, agg_panel, weight_two, *pieces)


def sum_everywhere(grads):
    shares = lax.all_to_all(grads.reshape(32, 16, FEAT), "row", 0, 0, tiled=True)
    share = jnp.sum(shares.astype(F32), 0).astype(BF16)
    shares = lax.all_to_all(
        jnp.broadcast_to(share, (GZ, 16, FEAT)), "col", 0, 0, tiled=True
    )
    share = jnp.sum(shares.astype(F32), 0).astype(BF16)
    full = lax.all_to_all(jnp.broadcast_to(share, (32, 16, FEAT)), "row", 0, 0, tiled=True)
    return full.reshape(512, FEAT)


def body(features, weight_one, weight_two, adj_tiles, tile_rows, tile_cols, tile_counts, labels):
    tiles = adj_tiles[0, 0]
    row_ids = tile_rows[0, 0]
    col_ids = tile_cols[0, 0]
    count = tile_counts[0, 0]
    z = lax.axis_index("col")
    node_total = ROWS * lax.axis_size("row") * lax.axis_size("col")
    weight_two = jnp.pad(weight_two, ((0, 0), (0, CPAD - CLASSES)))
    labels = labels.reshape(GZ, ROWS)
    place = jnp.full((1,), z, jnp.int32)
    offset = (row_ids // 2 - z) % GZ
    half = row_ids % 2
    rank = sum(jnp.where(offset == d, PLACE_OF_OFFSET[d], 0) for d in range(GZ))
    sources = source_slots(col_ids)
    forward = group_tiles(rank * 2 + half, sources, 64, count, 16, FWD, FWD_GROUPS, EARLY)
    reverse = group_tiles(sources, offset * 2 + half, 16, count, 64, BWD, BWD_GROUPS, 0)

    ready = (forward, labels, place, weight_two, tiles)
    forward, labels, place, weight_two, tiles = lax.optimization_barrier(ready)
    pieces, tiles = gather_row(features, functools.partial(hold_tiles, tiles))
    parts, _ = spread_and_reduce(
        aggregate_early_kernel,
        aggregate_late_kernel,
        "aggregate",
        forward,
        (tiles, *pieces),
        (),
        (TB, FEAT),
        (ROWS, FEAT),
    )
    pieces, _ = gather_row(middle(parts))
    nodes = ROWS * 2 * GX * GY
    parts, (agg_panel, hidden_t, slope_t) = spread_and_reduce(
        logits_early_kernel,
        logits_late_kernel,
        "partial_logits",
        forward,
        (tiles, weight_one, weight_two, *pieces),
        (
            jax.ShapeDtypeStruct((nodes, FEAT), BF16),
            jax.ShapeDtypeStruct((FEAT, nodes), BF16),
            jax.ShapeDtypeStruct((FEAT, nodes), BF16),
        ),
        (CPAD, TB),
        (CPAD, ROWS),
    )
    logits, grad_t = loss_grad(parts, labels, place, node_total ** (-0.5))
    grad_pieces = gather_col(grad_t)
    grads = backward(reverse, tiles, hidden_t, slope_t, agg_panel, weight_two, grad_pieces)
    grads = sum_everywhere(grads)
    grad_one = grads[:FEAT].astype(F32)
    grad_two = grads[FEAT:, :CLASSES].astype(F32)
    return logits, grad_one, grad_two


def solution(mesh):
    in_specs = (
        P(("row", "col"), None),
        P(),
        P(),
        P("row", "col", None, None, None),
        P("row", "col", None),
        P("row", "col", None),
        P("row", "col"),
        P("row"),
    )
    out_specs = (P(("row", "col"), None), P(), P())
    return jax.shard_map(body, mesh=mesh, in_specs=in_specs, out_specs=out_specs, check_vma=False)
```

```python
import functools

import jax
import jax.numpy as jnp
from jax import lax
from jax.experimental import pallas as pl
from jax.experimental.pallas import tpu as pltpu
from jax.sharding import PartitionSpec as P

F32 = jnp.float32
BF16 = jnp.bfloat16
NT = (((1,), (1,)), ((), ()))
NN = (((1,), (0,)), ((), ()))
TB = 128
GX, GY, GZ = 4, 4, 8
ROWS = 256
FEAT = 256
CLASSES = 172
CPAD = 176
SLOTS = 128
FWD = 4
BWD = 2
UNROLL = 4
FWD_GROUPS = 52
BWD_GROUPS = 136
CHUNK = 1024
EARLY = 6
PLACE_OF_OFFSET = (7, 3, 4, 0, 1, 2, 5, 6)


def params(mib):
    return pltpu.CompilerParams(vmem_limit_bytes=mib * 1024 * 1024)


def vmem_spec():
    return pl.BlockSpec(memory_space=pltpu.VMEM)


def hbm_spec():
    return pl.BlockSpec(memory_space=pltpu.HBM)


def smem_spec():
    return pl.BlockSpec(memory_space=pltpu.SMEM)


def hold_kernel(tiles_hbm, after, tiles, sem):
    copy = pltpu.make_async_copy(tiles_hbm, tiles, sem)
    copy.start()
    copy.wait()


def hold_tiles(tiles, after):
    return pl.pallas_call(
        hold_kernel,
        name="hold_tiles",
        out_shape=jax.ShapeDtypeStruct(tiles.shape, tiles.dtype),
        in_specs=[hbm_spec(), vmem_spec()],
        out_specs=vmem_spec(),
        scratch_shapes=[pltpu.SemaphoreType.DMA],
        compiler_params=params(4),
        cost_estimate=pl.CostEstimate(flops=0, bytes_accessed=10**3, transcendentals=0),
    )(tiles, after)


def row_perm(move):
    pairs = []
    for index in range(GX * GY * 2):
        x, y, core = index // (2 * GY), (index // 2) % GY, index % 2
        x, y, core = move(x, y, core)
        pairs.append((index, ((x % GX) * GY + y % GY) * 2 + core))
    return pairs


def first_axis(step):
    return row_perm(lambda x, y, c: (x, y + step, c) if c == 0 else (x + step, y, c))


def second_axis(step):
    return row_perm(lambda x, y, c: (x + step, y, c) if c == 0 else (x, y + step, c))


def swap_core():
    return row_perm(lambda x, y, c: (x, y, 1 - c))


def gather_row(own, beside, relay):
    send = lambda v, perm: lax.ppermute(v, "row", perm)
    line = jnp.concatenate(
        [
            own,
            send(own, first_axis(-1)),
            send(own, first_axis(2)),
            send(own, first_axis(1)),
        ],
        0,
    )
    half = line.shape[0] // 2
    plus = send(line, second_axis(-1))
    minus = send(line, second_axis(1))
    if relay:
        late = [send(minus[:half], second_axis(1)), send(plus[half:], second_axis(-1))]
        line, plus, minus = lax.optimization_barrier((line, plus, minus))
    else:
        late = [send(line, second_axis(2))]
        line, plus = lax.optimization_barrier((line, plus))
    early = [line, plus, minus]
    early = early + [send(v, swap_core()) for v in early]
    late[-1], done = lax.optimization_barrier((late[-1], beside(early)))
    return early, late + [send(v, swap_core()) for v in late], done


def source_slots(col_ids):
    me = lax.axis_index("row")
    device = col_ids >> 1
    dx = ((device >> 3) - (me >> 3)) & (GX - 1)
    dy = ((device >> 1) - (me >> 1)) & (GY - 1)
    other = device & 1
    along_first = jnp.where(other == 0, dy, dx)
    along_second = jnp.where(other == 0, dx, dy)
    swapped = (other ^ me) & 1
    early = (swapped * 3 + jnp.where(along_second == 3, 2, along_second)) * 4
    line = jnp.where(along_second == 2, 24 + swapped * 4, early)
    return (line + along_first) * 2 + (col_ids & 1)


def along_col(value, step):
    return lax.ppermute(value, "col", [(i, (i + step) % GZ) for i in range(GZ)])


def gather_col(own):
    near = {d: along_col(own, -d if d < 4 else GZ - d) for d in (2, 6, 1, 7)}
    up = jnp.concatenate([near[1], near[2][:, :TB]], 1)
    down = jnp.concatenate([near[6][:, TB:], near[7]], 1)
    up, down = along_col(up, -2), along_col(down, 2)
    return [own] + [near[d] for d in (1, 2, 6, 7)], up, down


def gradient_slots(offset, half):
    early = jnp.where(offset > 5, offset - 3, offset) * 2 + half
    late = offset * 2 + half + 4
    is_late = (offset >= 3) & (offset <= 5)
    return jnp.where(is_late, late, early), is_late.astype(jnp.int32)


def reduce_col(up, down, late):
    up, down = along_col(up, 2), along_col(down, -2)
    one, two, six, seven = late()
    width = one.shape[1]
    half = jnp.zeros((one.shape[0], width // 2), F32)
    extra_up = jnp.concatenate([up[:, width:].astype(F32), half], 1)
    extra_down = jnp.concatenate([half, down[:, width:].astype(F32)], 1)
    return [
        along_col((two + extra_up).astype(BF16), 2),
        along_col((six + extra_down).astype(BF16), -2),
        along_col((one + up[:, :width].astype(F32)).astype(BF16), 1),
        along_col((seven + down[:, :width].astype(F32)).astype(BF16), -1),
    ]


def group_tiles(target, source, empty, count, n_targets, group, n_groups, early):
    slots = jnp.arange(SLOTS, dtype=jnp.int32)
    live = slots < count
    key = jnp.where(live, target, n_targets)
    targets = jnp.arange(n_targets, dtype=jnp.int32)
    members = jnp.sum((key[None, :] == targets[:, None]).astype(jnp.int32), 1)
    groups = (members + group - 1) >> (group.bit_length() - 1)
    n_early = jnp.sum(jnp.where(targets < early, groups, 0))
    n_early = (n_early + UNROLL - 1) & -UNROLL
    n_all = n_early + jnp.sum(jnp.where(targets >= early, groups, 0))
    before = (targets[None, :] < key[:, None]) & (
        (targets[None, :] >= early) == (key[:, None] >= early)
    )
    earlier = jnp.sum(jnp.where(before, groups[None, :], 0), 1)
    earlier = earlier + jnp.where(key >= early, n_early, 0)
    rank = jnp.sum(
        ((key[None, :] == key[:, None]) & (slots[None, :] < slots[:, None])).astype(jnp.int32), 1
    )
    place = jnp.where(live, earlier * group + rank, -1)
    places = jnp.arange(n_groups * group, dtype=jnp.int32)
    hit = place[None, :] == places[:, None]
    order = jnp.sum(jnp.where(hit, slots[None, :], 0), 1)
    picked = empty + jnp.sum(jnp.where(hit, source[None, :] - empty, 0), 1)
    first = place[None, :] == group * jnp.arange(n_groups, dtype=jnp.int32)[:, None]
    goal = jnp.sum(jnp.where(first, target[None, :], 0), 1)
    counts = jnp.where(jnp.arange(2) == 0, n_early, n_all)
    return order, picked, goal, counts


def run_groups(table, group, first, last, shift, product, total):
    order, picked, goal, _ = table

    def step(i, carry):
        made = []
        for u in range(UNROLL):
            start = (i * UNROLL + u) * group
            tiles = [order[start + k] for k in range(group)]
            sources = [picked[start + k] for k in range(group)]
            made.append(product(tiles, sources))
        for u in range(UNROLL):
            total[jnp.maximum(goal[i * UNROLL + u] - shift, 0)] += made[u]
        return carry

    lax.fori_loop(first // UNROLL, (last + UNROLL - 1) // UNROLL, step, 0)


def clear(ref):
    def step(i, carry):
        ref[i] = jnp.zeros(ref.shape[1:], ref.dtype)
        return carry

    lax.fori_loop(0, ref.shape[0], step, 0)


def copy_rows(piece, panel, start, rows):
    def step(i, carry):
        origin = pl.ds(pl.multiple_of(i * rows, rows), rows)
        target = pl.ds(pl.multiple_of(start + i * rows, rows), rows)
        panel[target, :] = piece[origin, :]
        return carry

    lax.fori_loop(0, piece.shape[0] // rows, step, 0)


def rows_product(tiles, source):
    def product(picked, origins):
        return lax.dot_general(
            jnp.concatenate([tiles[t] for t in picked], 1),
            jnp.concatenate([source[o] for o in origins], 0),
            NN,
            preferred_element_type=F32,
        )

    return product


def columns_product(tiles, source):
    def product(picked, origins):
        return lax.dot_general(
            jnp.concatenate([source[o] for o in origins], 1),
            jnp.concatenate([tiles[t] for t in picked], 1),
            NT,
            preferred_element_type=F32,
        )

    return product


def halves_of_rows(total, place):
    return jnp.concatenate([total[2 * place], total[2 * place + 1]], 0)


def halves_of_columns(total, place):
    return jnp.concatenate([total[2 * place], total[2 * place + 1]], 1)


def early_outputs(total, whole, out_up, out_down):
    far = whole(total, 1)
    width = far.shape[1]
    out_up[:, :width] = whole(total, 0).astype(BF16)
    out_up[:, width:] = far[:, : width // 2].astype(BF16)
    out_down[:, :width] = whole(total, 2).astype(BF16)
    out_down[:, width:] = far[:, width // 2 :].astype(BF16)


def aggregate_early_kernel(*refs):
    table, (tiles, *rest) = refs[:4], refs[4:]
    pieces, (source, out_up, out_down, total) = rest[:-4], rest[-4:]
    filled = 0
    for piece in pieces:

        def step(i, carry):
            source[filled + i] = piece[pl.ds(pl.multiple_of(i * TB, TB), TB), :]
            return carry

        lax.fori_loop(0, piece.shape[0] // TB, step, 0)
        filled += piece.shape[0] // TB
    source[filled] = jnp.zeros((TB, FEAT), BF16)
    clear(total)
    run_groups(table, FWD, 0, table[3][0], 0, rows_product(tiles, source), total)
    early_outputs(total, halves_of_rows, out_up, out_down)


def aggregate_late_kernel(*refs):
    table, (tiles, source, *rest) = refs[:4], refs[4:]
    outs, total = rest[:5], rest[5]
    clear(total)
    run_groups(table, FWD, table[3][0], table[3][1], EARLY, rows_product(tiles, source), total)
    for place, out in enumerate(outs):
        out[...] = halves_of_rows(total, place)


def sigmoid(value):
    return 0.5 * jnp.tanh(0.5 * value) + 0.5


def gates(pieces, weight_one_t, weight_two_t, source, agg, hidden_t, slope_t):
    filled = 0
    for piece in pieces:
        copy_rows(piece, agg, filled, ROWS)
        filled += piece.shape[0]

    def step(i, carry):
        span = pl.ds(pl.multiple_of(i * CHUNK, CHUNK), CHUNK)
        pre = lax.dot_general(weight_one_t[...], agg[span, :], NT, preferred_element_type=F32)
        gate = sigmoid(pre)
        hidden = (pre * gate).astype(BF16)
        hidden_t[:, span] = hidden
        slope_t[:, span] = (gate * (1.0 + pre * (1.0 - gate))).astype(BF16)
        projected = lax.dot_general(
            weight_two_t[...], hidden, NN, preferred_element_type=F32
        ).astype(BF16)
        for block in range(CHUNK // TB):
            source[i * (CHUNK // TB) + block] = projected[:, block * TB : (block + 1) * TB]
        return carry

    lax.fori_loop(0, filled // CHUNK, step, 0)


def panel_shapes(nodes):
    return (
        jax.ShapeDtypeStruct((nodes, FEAT), BF16),
        jax.ShapeDtypeStruct((FEAT, nodes), BF16),
        jax.ShapeDtypeStruct((FEAT, nodes), BF16),
    )


def gates_kernel(weight_one_t, weight_two_t, *rest):
    gates(rest[:-4], weight_one_t, weight_two_t, *rest[-4:])


def early_gates(weight_one_t, weight_two_t, pieces):
    nodes = sum(p.shape[0] for p in pieces)
    return pl.pallas_call(
        gates_kernel,
        name="early_gates",
        out_shape=(
            jax.ShapeDtypeStruct((nodes // TB, CPAD, TB), BF16),
            *panel_shapes(nodes),
        ),
        in_specs=[vmem_spec()] * (2 + len(pieces)),
        out_specs=[vmem_spec()] * 4,
        compiler_params=params(8),
        cost_estimate=pl.CostEstimate(flops=10**3, bytes_accessed=10**3, transcendentals=0),
    )(weight_one_t, weight_two_t, *pieces)


def logits_early_kernel(*refs):
    table, (tiles, weight_one_t, weight_two_t, begun, *rest) = refs[:4], refs[4:]
    pieces, rest = rest[:-7], rest[-7:]
    source, out_up, out_down, agg, hidden_t, slope_t, total = rest
    blocks = begun.shape[0]

    def step(i, carry):
        source[i] = begun[i]
        return carry

    lax.fori_loop(0, blocks, step, 0)
    later = source.at[pl.ds(blocks, 64 - blocks)]
    gates(pieces, weight_one_t, weight_two_t, later, agg, hidden_t, slope_t)
    source[64] = jnp.zeros((CPAD, TB), BF16)
    clear(total)
    run_groups(table, FWD, 0, table[3][0], 0, columns_product(tiles, source), total)
    early_outputs(total, halves_of_columns, out_up, out_down)


def logits_late_kernel(*refs):
    table, (tiles, source, *rest) = refs[:4], refs[4:]
    outs, total = rest[:5], rest[5]
    clear(total)
    run_groups(table, FWD, table[3][0], table[3][1], EARLY, columns_product(tiles, source), total)
    for place, out in enumerate(outs):
        out[...] = halves_of_columns(total, place)


def spread_and_reduce(early_kernel, late_kernel, name, table, operands, kept, block, out):
    cost = pl.CostEstimate(flops=10**9, bytes_accessed=10**7, transcendentals=0)
    wide = jax.ShapeDtypeStruct((out[0], out[1] * 3 // 2), BF16)
    source, up, down, *kept = pl.pallas_call(
        early_kernel,
        name=name + "_early",
        out_shape=(jax.ShapeDtypeStruct((65, *block), BF16), wide, wide, *kept),
        in_specs=[smem_spec()] * 4 + [vmem_spec()] * len(operands),
        out_specs=[vmem_spec()] * (3 + len(kept)),
        scratch_shapes=[pltpu.VMEM((EARLY, *block), F32)],
        compiler_params=params(10),
        cost_estimate=cost,
    )(*table, *operands)
    *late, own = pl.pallas_call(
        late_kernel,
        name=name + "_late",
        out_shape=(jax.ShapeDtypeStruct(out, F32),) * 5,
        in_specs=[smem_spec()] * 4 + [vmem_spec()] * 2,
        out_specs=[vmem_spec()] * 5,
        scratch_shapes=[pltpu.VMEM((16 - EARLY, *block), F32)],
        compiler_params=params(8),
        cost_estimate=cost,
    )(*table, operands[0], source)
    return [own] + reduce_col(up, down, lambda: late), kept


def add_up(parts):
    summed = parts[0][...].astype(F32)
    for part in parts[1:]:
        summed += part[...].astype(F32)
    return summed


def middle_kernel(*refs):
    parts, (one, two_t, agg, one_t, wide_t, wide, padded) = refs[:5], refs[5:]
    agg[...] = add_up(parts).astype(BF16)
    one_t[...] = jnp.transpose(one[...].astype(F32)).astype(BF16)
    padded[...] = jnp.zeros_like(padded)
    padded[0:CLASSES] = two_t[...].astype(F32)
    wide_t[...] = padded[...].astype(BF16)
    wide[...] = jnp.transpose(padded[...]).astype(BF16)


def middle(parts, weight_one, weight_two_t):
    return pl.pallas_call(
        middle_kernel,
        name="middle",
        out_shape=(
            jax.ShapeDtypeStruct((ROWS, FEAT), BF16),
            jax.ShapeDtypeStruct((FEAT, FEAT), BF16),
            jax.ShapeDtypeStruct((CPAD, FEAT), BF16),
            jax.ShapeDtypeStruct((FEAT, CPAD), BF16),
        ),
        in_specs=[vmem_spec()] * 7,
        out_specs=[vmem_spec()] * 4,
        scratch_shapes=[pltpu.VMEM((CPAD, FEAT), F32)],
        compiler_params=params(8),
    )(*parts, weight_one, weight_two_t)


def loss_kernel(scale, *refs):
    parts, (labels, place, logits_t, grad_t) = refs[:5], refs[5:]
    summed = add_up(parts)
    logits_t[...] = summed[:CLASSES]
    ids = lax.broadcasted_iota(jnp.int32, summed.shape, 0)
    valid = ids < CLASSES
    top = jnp.max(jnp.where(valid, summed, -jnp.inf), 0, keepdims=True)
    grown = jnp.where(valid, jnp.exp(summed - top), 0.0)
    soft = grown / jnp.sum(grown, 0, keepdims=True)
    own_labels = jnp.concatenate([labels[pl.ds(place[0] * 2 + k, 1), :] for k in range(2)], 1)
    onehot = (ids == own_labels).astype(F32)
    grad_t[...] = ((soft - onehot) * scale).astype(BF16)


def loss_grad(parts, labels, place, scale):
    return pl.pallas_call(
        functools.partial(loss_kernel, scale),
        name="loss_grad",
        out_shape=(
            jax.ShapeDtypeStruct((CLASSES, ROWS), F32),
            jax.ShapeDtypeStruct((CPAD, ROWS), BF16),
        ),
        in_specs=[vmem_spec()] * 6 + [smem_spec()],
        out_specs=[vmem_spec()] * 2,
        compiler_params=params(8),
    )(*parts, labels, place)


def backward_tiles(table, first, last, shift, tiles, grads, total):
    def product(picked, origins):
        return lax.dot_general(
            jnp.concatenate([grads[o] for o in origins], 1),
            jnp.concatenate([tiles[t] for t in picked], 0),
            NN,
            preferred_element_type=F32,
        )

    run_groups(table, BWD, first, last, shift, product, total)


def backward_early_kernel(*refs):
    table, (tiles, *pieces), (total, grads) = refs[:4], refs[4:-2], refs[-2:]
    for place, piece in enumerate(pieces):
        grads[2 * place] = piece[:, :TB]
        grads[2 * place + 1] = piece[:, TB:]
    grads[16] = jnp.zeros((CPAD, TB), BF16)
    clear(total)
    backward_tiles(table, 0, table[3][0], 0, tiles, grads, total)


def backward_early(table, tiles, pieces):
    return pl.pallas_call(
        backward_early_kernel,
        name="backward_early",
        out_shape=jax.ShapeDtypeStruct((64, CPAD, TB), F32),
        in_specs=[smem_spec()] * 4 + [vmem_spec()] * (1 + len(pieces)),
        out_specs=vmem_spec(),
        scratch_shapes=[pltpu.VMEM((17, CPAD, TB), BF16)],
        compiler_params=params(8),
        cost_estimate=pl.CostEstimate(flops=10**3, bytes_accessed=10**3, transcendentals=0),
    )(*table, tiles, *pieces)


def backward_late_kernel(*refs):
    table, (tiles, weight_two, begun, *rest) = refs[:4], refs[4:]
    panels, (up, down, *rest) = (rest[0:3], rest[3:6]), rest[6:]
    out, grads, total, sum_one, sum_two = rest
    for place, piece in enumerate((up, down)):
        for k in range(3):
            grads[10 + 3 * place + k] = piece[:, k * TB : (k + 1) * TB]
    grads[16] = jnp.zeros((CPAD, TB), BF16)

    def take(i, carry):
        total[i] = begun[i]
        return carry

    lax.fori_loop(0, 64, take, 0)
    backward_tiles(table, table[3][0], table[3][1], 64, tiles, grads, total)
    sum_one[...] = jnp.zeros_like(sum_one)
    sum_two[...] = jnp.zeros_like(sum_two)
    blocks = 8
    span = blocks * TB
    done = 0
    for agg, hidden, slope in panels:

        def finish(i, carry):
            held = [total[done + i * blocks + k] for k in range(blocks)]
            back = jnp.concatenate(held, 1).astype(BF16)
            part = pl.ds(pl.multiple_of(i * span, span), span)
            grad = lax.dot_general(weight_two[...], back, NN, preferred_element_type=F32)
            grad = (grad * slope[:, part].astype(F32)).astype(BF16)
            sum_one[...] += lax.dot_general(grad, agg[part, :], NN, preferred_element_type=F32)
            sum_two[...] += lax.dot_general(back, hidden[:, part], NT, preferred_element_type=F32)
            return carry

        lax.fori_loop(0, agg.shape[0] // span, finish, 0)
        done += agg.shape[0] // TB
    out[0:FEAT] = jnp.transpose(sum_one[...]).astype(BF16)
    out[FEAT : FEAT + CPAD] = sum_two[...].astype(BF16)
    out[FEAT + CPAD :] = jnp.zeros((512 - FEAT - CPAD, FEAT), BF16)


def backward_late(table, tiles, weight_two, begun, panels, up, down):
    return pl.pallas_call(
        backward_late_kernel,
        name="backward_late",
        out_shape=jax.ShapeDtypeStruct((512, FEAT), BF16),
        in_specs=[smem_spec()] * 4 + [vmem_spec()] * (5 + len(panels)),
        out_specs=vmem_spec(),
        scratch_shapes=[
            pltpu.VMEM((17, CPAD, TB), BF16),
            pltpu.VMEM((64, CPAD, TB), F32),
            pltpu.VMEM((FEAT, FEAT), F32),
            pltpu.VMEM((CPAD, FEAT), F32),
        ],
        compiler_params=params(12),
        cost_estimate=pl.CostEstimate(flops=5 * 10**9, bytes_accessed=2 * 10**7, transcendentals=0),
    )(*table, tiles, weight_two, begun, *panels, up, down)


def sum_everywhere(grads):
    shares = lax.all_to_all(grads.reshape(32, 16, FEAT), "row", 0, 0, tiled=True)
    share = jnp.sum(shares.astype(F32), 0).astype(BF16)
    shares = lax.all_to_all(
        jnp.broadcast_to(share, (GZ, 16, FEAT)), "col", 0, 0, tiled=True
    )
    share = jnp.sum(shares.astype(F32), 0).astype(BF16)
    full = lax.all_to_all(jnp.broadcast_to(share, (32, 16, FEAT)), "row", 0, 0, tiled=True)
    return full.reshape(512, FEAT)


def body(features, weight_one, weight_two, adj_tiles, tile_rows, tile_cols, tile_counts, labels):
    z = lax.axis_index("col")
    node_total = ROWS * lax.axis_size("row") * lax.axis_size("col")
    labels = labels.reshape(GZ * ROWS // TB, TB)
    place = jnp.full((1,), z, jnp.int32)
    second_t = weight_two.T

    def prepare(early):
        given = (tile_rows[0, 0], tile_cols[0, 0], tile_counts[0, 0], early[0])
        row_ids, col_ids, count, _ = lax.optimization_barrier(given)
        offset = ((row_ids >> 1) - z) & (GZ - 1)
        half = row_ids & 1
        rank = sum(jnp.where(offset == d, PLACE_OF_OFFSET[d], 0) for d in range(GZ))
        sources = source_slots(col_ids)
        forward = group_tiles(rank * 2 + half, sources, 64, count, 16, FWD, FWD_GROUPS, EARLY)
        slots, late = gradient_slots(offset, half)
        reverse = group_tiles(late * 64 + sources, slots, 16, count, 128, BWD, BWD_GROUPS, 64)
        ready = (forward, reverse, labels, place, adj_tiles[0, 0])
        *ready, tiles = lax.optimization_barrier(ready)
        return (*ready, hold_tiles(tiles, early[0]))

    early, late, done = gather_row(features, prepare, False)
    forward, reverse, labels, place, tiles = done
    parts, _ = spread_and_reduce(
        aggregate_early_kernel,
        aggregate_late_kernel,
        "aggregate",
        forward,
        (tiles, *early, *late),
        (),
        (TB, FEAT),
        (ROWS, FEAT),
    )
    agg, weight_one_t, weight_two_t, weight_two = middle(parts, weight_one, second_t)
    early, late, begun = gather_row(
        agg, functools.partial(early_gates, weight_one_t, weight_two_t), True
    )
    parts, panel = spread_and_reduce(
        logits_early_kernel,
        logits_late_kernel,
        "partial_logits",
        forward,
        (tiles, weight_one_t, weight_two_t, begun[0], *late),
        panel_shapes(sum(p.shape[0] for p in late)),
        (CPAD, TB),
        (CPAD, ROWS),
    )
    logits_t, grad_t = loss_grad(parts, labels, place, node_total ** (-0.5))
    near, up, down = gather_col(grad_t)
    total = backward_early(reverse, tiles, near)
    grads = backward_late(
        reverse, tiles, weight_two, total, (*begun[1:], *panel), up, down
    )
    grads = sum_everywhere(grads)
    grad_one = grads[:FEAT].astype(F32)
    grad_two = grads[FEAT : FEAT + CLASSES].astype(F32).T
    return logits_t.T, grad_one, grad_two


def solution(mesh):
    in_specs = (
        P(("row", "col"), None),
        P(),
        P(),
        P("row", "col", None, None, None),
        P("row", "col", None),
        P("row", "col", None),
        P("row", "col"),
        P("row"),
    )
    out_specs = (P(("row", "col"), None), P(), P())
    return jax.shard_map(body, mesh=mesh, in_specs=in_specs, out_specs=out_specs, check_vma=False)
```

```python
import functools

import jax
import jax.numpy as jnp
from jax import lax
from jax.experimental import pallas as pl
from jax.experimental.pallas import tpu as pltpu
from jax.sharding import PartitionSpec as P

F32 = jnp.float32
BF16 = jnp.bfloat16
NT = (((1,), (1,)), ((), ()))
NN = (((1,), (0,)), ((), ()))
TB = 128
GX, GY, GZ = 4, 4, 8
ROWS = 256
FEAT = 256
CLASSES = 172
CPAD = 176
SLOTS = 128
FWD = 4
BWD = 2
UNROLL = 4
FWD_GROUPS = 52
BWD_GROUPS = 136
CHUNK = 1024
EARLY = 6
PLACE_OF_OFFSET = (7, 3, 4, 0, 1, 2, 5, 6)


def params(mib):
    return pltpu.CompilerParams(vmem_limit_bytes=mib * 1024 * 1024)


def vmem_spec():
    return pl.BlockSpec(memory_space=pltpu.VMEM)


def hbm_spec():
    return pl.BlockSpec(memory_space=pltpu.HBM)


def smem_spec():
    return pl.BlockSpec(memory_space=pltpu.SMEM)


def hold_kernel(tiles_hbm, after, tiles, sem):
    copy = pltpu.make_async_copy(tiles_hbm, tiles, sem)
    copy.start()
    copy.wait()


def hold_tiles(tiles, after):
    return pl.pallas_call(
        hold_kernel,
        name="hold_tiles",
        out_shape=jax.ShapeDtypeStruct(tiles.shape, tiles.dtype),
        in_specs=[hbm_spec(), vmem_spec()],
        out_specs=vmem_spec(),
        scratch_shapes=[pltpu.SemaphoreType.DMA],
        compiler_params=params(4),
        cost_estimate=pl.CostEstimate(flops=0, bytes_accessed=10**3, transcendentals=0),
    )(tiles, after)


def row_perm(move):
    pairs = []
    for index in range(GX * GY * 2):
        x, y, core = index // (2 * GY), (index // 2) % GY, index % 2
        x, y, core = move(x, y, core)
        pairs.append((index, ((x % GX) * GY + y % GY) * 2 + core))
    return pairs


def first_axis(step):
    return row_perm(lambda x, y, c: (x, y + step, c) if c == 0 else (x + step, y, c))


def second_axis(step):
    return row_perm(lambda x, y, c: (x + step, y, c) if c == 0 else (x, y + step, c))


def swap_core():
    return row_perm(lambda x, y, c: (x, y, 1 - c))


def gather_row(own, beside):
    send = lambda v, perm: lax.ppermute(v, "row", perm)
    line = jnp.concatenate(
        [
            own,
            send(own, first_axis(-1)),
            send(own, first_axis(2)),
            send(own, first_axis(1)),
        ],
        0,
    )
    plus = send(line, second_axis(-1))
    minus = send(line, second_axis(1))
    two = send(line, second_axis(2))
    line, plus = lax.optimization_barrier((line, plus))
    early = [line, plus, minus]
    swapped = [send(v, swap_core()) for v in early]
    two, done = lax.optimization_barrier((two, beside(early)))
    return early, [two] + swapped + [send(two, swap_core())], done


def source_slots(col_ids):
    me = lax.axis_index("row")
    device = col_ids >> 1
    dx = ((device >> 3) - (me >> 3)) & (GX - 1)
    dy = ((device >> 1) - (me >> 1)) & (GY - 1)
    other = device & 1
    along_first = jnp.where(other == 0, dy, dx)
    along_second = jnp.where(other == 0, dx, dy)
    line = jnp.where(along_second > 1, 5 - along_second, along_second)
    line = ((other ^ me) & 1) * 4 + line
    return (line * 4 + along_first) * 2 + (col_ids & 1)


def along_col(value, step):
    return lax.ppermute(value, "col", [(i, (i + step) % GZ) for i in range(GZ)])


def gather_col(own):
    near = {d: along_col(own, -d if d < 4 else GZ - d) for d in (2, 6, 1, 7)}
    up = jnp.concatenate([near[1], near[2][:, :TB]], 1)
    down = jnp.concatenate([near[6][:, TB:], near[7]], 1)
    up, down = along_col(up, -2), along_col(down, 2)
    return [own] + [near[d] for d in (1, 2, 6, 7)], up, down


def gradient_slots(offset, half):
    early = jnp.where(offset > 5, offset - 3, offset) * 2 + half
    late = offset * 2 + half + 4
    is_late = (offset >= 3) & (offset <= 5)
    return jnp.where(is_late, late, early), is_late.astype(jnp.int32)


def reduce_col(up, down, late):
    up, down = along_col(up, 2), along_col(down, -2)
    one, two, six, seven = late()
    width = one.shape[1]
    half = jnp.zeros((one.shape[0], width // 2), F32)
    extra_up = jnp.concatenate([up[:, width:].astype(F32), half], 1)
    extra_down = jnp.concatenate([half, down[:, width:].astype(F32)], 1)
    return [
        along_col((two + extra_up).astype(BF16), 2),
        along_col((six + extra_down).astype(BF16), -2),
        along_col((one + up[:, :width].astype(F32)).astype(BF16), 1),
        along_col((seven + down[:, :width].astype(F32)).astype(BF16), -1),
    ]


def group_tiles(target, source, empty, count, n_targets, group, n_groups, early):
    slots = jnp.arange(SLOTS, dtype=jnp.int32)
    live = slots < count
    key = jnp.where(live, target, n_targets)
    targets = jnp.arange(n_targets, dtype=jnp.int32)
    members = jnp.sum((key[None, :] == targets[:, None]).astype(jnp.int32), 1)
    groups = (members + group - 1) >> (group.bit_length() - 1)
    n_early = jnp.sum(jnp.where(targets < early, groups, 0))
    n_early = (n_early + UNROLL - 1) & -UNROLL
    n_all = n_early + jnp.sum(jnp.where(targets >= early, groups, 0))
    before = (targets[None, :] < key[:, None]) & (
        (targets[None, :] >= early) == (key[:, None] >= early)
    )
    earlier = jnp.sum(jnp.where(before, groups[None, :], 0), 1)
    earlier = earlier + jnp.where(key >= early, n_early, 0)
    rank = jnp.sum(
        ((key[None, :] == key[:, None]) & (slots[None, :] < slots[:, None])).astype(jnp.int32), 1
    )
    place = jnp.where(live, earlier * group + rank, -1)
    places = jnp.arange(n_groups * group, dtype=jnp.int32)
    hit = place[None, :] == places[:, None]
    order = jnp.sum(jnp.where(hit, slots[None, :], 0), 1)
    picked = empty + jnp.sum(jnp.where(hit, source[None, :] - empty, 0), 1)
    first = place[None, :] == group * jnp.arange(n_groups, dtype=jnp.int32)[:, None]
    goal = jnp.sum(jnp.where(first, target[None, :], 0), 1)
    counts = jnp.where(jnp.arange(2) == 0, n_early, n_all)
    return order, picked, goal, counts


def run_groups(table, group, first, last, shift, product, total):
    order, picked, goal, _ = table

    def step(i, carry):
        made = []
        for u in range(UNROLL):
            start = (i * UNROLL + u) * group
            tiles = [order[start + k] for k in range(group)]
            sources = [picked[start + k] for k in range(group)]
            made.append(product(tiles, sources))
        for u in range(UNROLL):
            total[jnp.maximum(goal[i * UNROLL + u] - shift, 0)] += made[u]
        return carry

    lax.fori_loop(first // UNROLL, (last + UNROLL - 1) // UNROLL, step, 0)


def clear(ref):
    def step(i, carry):
        ref[i] = jnp.zeros(ref.shape[1:], ref.dtype)
        return carry

    lax.fori_loop(0, ref.shape[0], step, 0)


def copy_rows(piece, panel, start, rows):
    def step(i, carry):
        origin = pl.ds(pl.multiple_of(i * rows, rows), rows)
        target = pl.ds(pl.multiple_of(start + i * rows, rows), rows)
        panel[target, :] = piece[origin, :]
        return carry

    lax.fori_loop(0, piece.shape[0] // rows, step, 0)


def rows_product(tiles, source):
    def product(picked, origins):
        return lax.dot_general(
            jnp.concatenate([tiles[t] for t in picked], 1),
            jnp.concatenate([source[o] for o in origins], 0),
            NN,
            preferred_element_type=F32,
        )

    return product


def columns_product(tiles, source):
    def product(picked, origins):
        return lax.dot_general(
            jnp.concatenate([source[o] for o in origins], 1),
            jnp.concatenate([tiles[t] for t in picked], 1),
            NT,
            preferred_element_type=F32,
        )

    return product


def halves_of_rows(total, place):
    return jnp.concatenate([total[2 * place], total[2 * place + 1]], 0)


def halves_of_columns(total, place):
    return jnp.concatenate([total[2 * place], total[2 * place + 1]], 1)


def early_outputs(total, whole, out_up, out_down):
    far = whole(total, 1)
    width = far.shape[1]
    out_up[:, :width] = whole(total, 0).astype(BF16)
    out_up[:, width:] = far[:, : width // 2].astype(BF16)
    out_down[:, :width] = whole(total, 2).astype(BF16)
    out_down[:, width:] = far[:, width // 2 :].astype(BF16)


def aggregate_early_kernel(*refs):
    table, (tiles, *rest) = refs[:4], refs[4:]
    pieces, (source, out_up, out_down, total) = rest[:-4], rest[-4:]
    filled = 0
    for piece in pieces:

        def step(i, carry):
            source[filled + i] = piece[pl.ds(pl.multiple_of(i * TB, TB), TB), :]
            return carry

        lax.fori_loop(0, piece.shape[0] // TB, step, 0)
        filled += piece.shape[0] // TB
    source[filled] = jnp.zeros((TB, FEAT), BF16)
    clear(total)
    run_groups(table, FWD, 0, table[3][0], 0, rows_product(tiles, source), total)
    early_outputs(total, halves_of_rows, out_up, out_down)


def aggregate_late_kernel(*refs):
    table, (tiles, source, *rest) = refs[:4], refs[4:]
    outs, total = rest[:5], rest[5]
    clear(total)
    run_groups(table, FWD, table[3][0], table[3][1], EARLY, rows_product(tiles, source), total)
    for place, out in enumerate(outs):
        out[...] = halves_of_rows(total, place)


def sigmoid(value):
    return 0.5 * jnp.tanh(0.5 * value) + 0.5


def gates(pieces, weight_one_t, weight_two_t, source, agg, hidden_t, slope_t):
    filled = 0
    for piece in pieces:
        copy_rows(piece, agg, filled, ROWS)
        filled += piece.shape[0]

    def step(i, carry):
        span = pl.ds(pl.multiple_of(i * CHUNK, CHUNK), CHUNK)
        pre = lax.dot_general(weight_one_t[...], agg[span, :], NT, preferred_element_type=F32)
        gate = sigmoid(pre)
        hidden = (pre * gate).astype(BF16)
        hidden_t[:, span] = hidden
        slope_t[:, span] = (gate * (1.0 + pre * (1.0 - gate))).astype(BF16)
        projected = lax.dot_general(
            weight_two_t[...], hidden, NN, preferred_element_type=F32
        ).astype(BF16)
        for block in range(CHUNK // TB):
            source[i * (CHUNK // TB) + block] = projected[:, block * TB : (block + 1) * TB]
        return carry

    lax.fori_loop(0, filled // CHUNK, step, 0)


def panel_shapes(nodes):
    return (
        jax.ShapeDtypeStruct((nodes, FEAT), BF16),
        jax.ShapeDtypeStruct((FEAT, nodes), BF16),
        jax.ShapeDtypeStruct((FEAT, nodes), BF16),
    )


def gates_kernel(weight_one_t, weight_two_t, *rest):
    gates(rest[:-4], weight_one_t, weight_two_t, *rest[-4:])


def early_gates(weight_one_t, weight_two_t, pieces):
    nodes = sum(p.shape[0] for p in pieces)
    return pl.pallas_call(
        gates_kernel,
        name="early_gates",
        out_shape=(
            jax.ShapeDtypeStruct((nodes // TB, CPAD, TB), BF16),
            *panel_shapes(nodes),
        ),
        in_specs=[vmem_spec()] * (2 + len(pieces)),
        out_specs=[vmem_spec()] * 4,
        compiler_params=params(8),
        cost_estimate=pl.CostEstimate(flops=10**3, bytes_accessed=10**3, transcendentals=0),
    )(weight_one_t, weight_two_t, *pieces)


def logits_early_kernel(*refs):
    table, (tiles, weight_one_t, weight_two_t, begun, *rest) = refs[:4], refs[4:]
    pieces, rest = rest[:-7], rest[-7:]
    source, out_up, out_down, agg, hidden_t, slope_t, total = rest
    blocks = begun.shape[0]

    def step(i, carry):
        source[i] = begun[i]
        return carry

    lax.fori_loop(0, blocks, step, 0)
    later = source.at[pl.ds(blocks, 64 - blocks)]
    gates(pieces, weight_one_t, weight_two_t, later, agg, hidden_t, slope_t)
    source[64] = jnp.zeros((CPAD, TB), BF16)
    clear(total)
    run_groups(table, FWD, 0, table[3][0], 0, columns_product(tiles, source), total)
    early_outputs(total, halves_of_columns, out_up, out_down)


def logits_late_kernel(*refs):
    table, (tiles, source, *rest) = refs[:4], refs[4:]
    outs, total = rest[:5], rest[5]
    clear(total)
    run_groups(table, FWD, table[3][0], table[3][1], EARLY, columns_product(tiles, source), total)
    for place, out in enumerate(outs):
        out[...] = halves_of_columns(total, place)


def spread_and_reduce(early_kernel, late_kernel, name, table, operands, kept, block, out):
    cost = pl.CostEstimate(flops=10**9, bytes_accessed=10**7, transcendentals=0)
    wide = jax.ShapeDtypeStruct((out[0], out[1] * 3 // 2), BF16)
    source, up, down, *kept = pl.pallas_call(
        early_kernel,
        name=name + "_early",
        out_shape=(jax.ShapeDtypeStruct((65, *block), BF16), wide, wide, *kept),
        in_specs=[smem_spec()] * 4 + [vmem_spec()] * len(operands),
        out_specs=[vmem_spec()] * (3 + len(kept)),
        scratch_shapes=[pltpu.VMEM((EARLY, *block), F32)],
        compiler_params=params(10),
        cost_estimate=cost,
    )(*table, *operands)
    *late, own = pl.pallas_call(
        late_kernel,
        name=name + "_late",
        out_shape=(jax.ShapeDtypeStruct(out, F32),) * 5,
        in_specs=[smem_spec()] * 4 + [vmem_spec()] * 2,
        out_specs=[vmem_spec()] * 5,
        scratch_shapes=[pltpu.VMEM((16 - EARLY, *block), F32)],
        compiler_params=params(8),
        cost_estimate=cost,
    )(*table, operands[0], source)
    return [own] + reduce_col(up, down, lambda: late), kept


def add_up(parts):
    summed = parts[0][...].astype(F32)
    for part in parts[1:]:
        summed += part[...].astype(F32)
    return summed


def middle_kernel(*refs):
    parts, (one, two_t, agg, one_t, wide_t, wide, padded) = refs[:5], refs[5:]
    agg[...] = add_up(parts).astype(BF16)
    one_t[...] = jnp.transpose(one[...].astype(F32)).astype(BF16)
    padded[...] = jnp.zeros_like(padded)
    padded[0:CLASSES] = two_t[...].astype(F32)
    wide_t[...] = padded[...].astype(BF16)
    wide[...] = jnp.transpose(padded[...]).astype(BF16)


def middle(parts, weight_one, weight_two_t):
    return pl.pallas_call(
        middle_kernel,
        name="middle",
        out_shape=(
            jax.ShapeDtypeStruct((ROWS, FEAT), BF16),
            jax.ShapeDtypeStruct((FEAT, FEAT), BF16),
            jax.ShapeDtypeStruct((CPAD, FEAT), BF16),
            jax.ShapeDtypeStruct((FEAT, CPAD), BF16),
        ),
        in_specs=[vmem_spec()] * 7,
        out_specs=[vmem_spec()] * 4,
        scratch_shapes=[pltpu.VMEM((CPAD, FEAT), F32)],
        compiler_params=params(8),
    )(*parts, weight_one, weight_two_t)


def loss_kernel(scale, *refs):
    parts, (labels, place, logits_t, grad_t) = refs[:5], refs[5:]
    summed = add_up(parts)
    logits_t[...] = summed[:CLASSES]
    ids = lax.broadcasted_iota(jnp.int32, summed.shape, 0)
    valid = ids < CLASSES
    top = jnp.max(jnp.where(valid, summed, -jnp.inf), 0, keepdims=True)
    grown = jnp.where(valid, jnp.exp(summed - top), 0.0)
    soft = grown / jnp.sum(grown, 0, keepdims=True)
    own_labels = jnp.concatenate([labels[pl.ds(place[0] * 2 + k, 1), :] for k in range(2)], 1)
    onehot = (ids == own_labels).astype(F32)
    grad_t[...] = ((soft - onehot) * scale).astype(BF16)


def loss_grad(parts, labels, place, scale):
    return pl.pallas_call(
        functools.partial(loss_kernel, scale),
        name="loss_grad",
        out_shape=(
            jax.ShapeDtypeStruct((CLASSES, ROWS), F32),
            jax.ShapeDtypeStruct((CPAD, ROWS), BF16),
        ),
        in_specs=[vmem_spec()] * 6 + [smem_spec()],
        out_specs=[vmem_spec()] * 2,
        compiler_params=params(8),
    )(*parts, labels, place)


def backward_tiles(table, first, last, shift, tiles, grads, total):
    def product(picked, origins):
        return lax.dot_general(
            jnp.concatenate([grads[o] for o in origins], 1),
            jnp.concatenate([tiles[t] for t in picked], 0),
            NN,
            preferred_element_type=F32,
        )

    run_groups(table, BWD, first, last, shift, product, total)


def backward_early_kernel(*refs):
    table, (tiles, *pieces), (total, grads) = refs[:4], refs[4:-2], refs[-2:]
    for place, piece in enumerate(pieces):
        grads[2 * place] = piece[:, :TB]
        grads[2 * place + 1] = piece[:, TB:]
    grads[16] = jnp.zeros((CPAD, TB), BF16)
    clear(total)
    backward_tiles(table, 0, table[3][0], 0, tiles, grads, total)


def backward_early(table, tiles, pieces):
    return pl.pallas_call(
        backward_early_kernel,
        name="backward_early",
        out_shape=jax.ShapeDtypeStruct((64, CPAD, TB), F32),
        in_specs=[smem_spec()] * 4 + [vmem_spec()] * (1 + len(pieces)),
        out_specs=vmem_spec(),
        scratch_shapes=[pltpu.VMEM((17, CPAD, TB), BF16)],
        compiler_params=params(8),
        cost_estimate=pl.CostEstimate(flops=10**3, bytes_accessed=10**3, transcendentals=0),
    )(*table, tiles, *pieces)


def backward_late_kernel(*refs):
    table, (tiles, weight_two, begun, *rest) = refs[:4], refs[4:]
    panels, (up, down, *rest) = (rest[0:3], rest[3:6]), rest[6:]
    out, grads, total, sum_one, sum_two = rest
    for place, piece in enumerate((up, down)):
        for k in range(3):
            grads[10 + 3 * place + k] = piece[:, k * TB : (k + 1) * TB]
    grads[16] = jnp.zeros((CPAD, TB), BF16)

    def take(i, carry):
        total[i] = begun[i]
        return carry

    lax.fori_loop(0, 64, take, 0)
    backward_tiles(table, table[3][0], table[3][1], 64, tiles, grads, total)
    sum_one[...] = jnp.zeros_like(sum_one)
    sum_two[...] = jnp.zeros_like(sum_two)
    blocks = 8
    span = blocks * TB
    done = 0
    for agg, hidden, slope in panels:

        def finish(i, carry):
            held = [total[done + i * blocks + k] for k in range(blocks)]
            back = jnp.concatenate(held, 1).astype(BF16)
            part = pl.ds(pl.multiple_of(i * span, span), span)
            grad = lax.dot_general(weight_two[...], back, NN, preferred_element_type=F32)
            grad = (grad * slope[:, part].astype(F32)).astype(BF16)
            sum_one[...] += lax.dot_general(grad, agg[part, :], NN, preferred_element_type=F32)
            sum_two[...] += lax.dot_general(back, hidden[:, part], NT, preferred_element_type=F32)
            return carry

        lax.fori_loop(0, agg.shape[0] // span, finish, 0)
        done += agg.shape[0] // TB
    out[0:FEAT] = jnp.transpose(sum_one[...]).astype(BF16)
    out[FEAT : FEAT + CPAD] = sum_two[...].astype(BF16)
    out[FEAT + CPAD :] = jnp.zeros((512 - FEAT - CPAD, FEAT), BF16)


def backward_late(table, tiles, weight_two, begun, panels, up, down):
    return pl.pallas_call(
        backward_late_kernel,
        name="backward_late",
        out_shape=jax.ShapeDtypeStruct((512, FEAT), BF16),
        in_specs=[smem_spec()] * 4 + [vmem_spec()] * (5 + len(panels)),
        out_specs=vmem_spec(),
        scratch_shapes=[
            pltpu.VMEM((17, CPAD, TB), BF16),
            pltpu.VMEM((64, CPAD, TB), F32),
            pltpu.VMEM((FEAT, FEAT), F32),
            pltpu.VMEM((CPAD, FEAT), F32),
        ],
        compiler_params=params(12),
        cost_estimate=pl.CostEstimate(flops=5 * 10**9, bytes_accessed=2 * 10**7, transcendentals=0),
    )(*table, tiles, weight_two, begun, *panels, up, down)


def sum_everywhere(grads):
    shares = lax.all_to_all(grads.reshape(32, 16, FEAT), "row", 0, 0, tiled=True)
    share = jnp.sum(shares.astype(F32), 0).astype(BF16)
    shares = lax.all_to_all(
        jnp.broadcast_to(share, (GZ, 16, FEAT)), "col", 0, 0, tiled=True
    )
    share = jnp.sum(shares.astype(F32), 0).astype(BF16)
    full = lax.all_to_all(jnp.broadcast_to(share, (32, 16, FEAT)), "row", 0, 0, tiled=True)
    return full.reshape(512, FEAT)


def unpack_kernel(grads, grad_one, grad_two_t):
    grad_one[...] = grads[0:FEAT].astype(F32)
    grad_two_t[...] = grads[FEAT : FEAT + CPAD].astype(F32)[:CLASSES]


def unpack(grads):
    return pl.pallas_call(
        unpack_kernel,
        name="unpack",
        out_shape=(
            jax.ShapeDtypeStruct((FEAT, FEAT), F32),
            jax.ShapeDtypeStruct((CLASSES, FEAT), F32),
        ),
        in_specs=[vmem_spec()],
        out_specs=[vmem_spec()] * 2,
        compiler_params=params(4),
    )(grads)


def body(features, weight_one, weight_two, adj_tiles, tile_rows, tile_cols, tile_counts, labels):
    z = lax.axis_index("col")
    node_total = ROWS * lax.axis_size("row") * lax.axis_size("col")
    labels = labels.reshape(GZ * ROWS // TB, TB)
    place = jnp.full((1,), z, jnp.int32)
    second_t = weight_two.T

    def prepare(early):
        given = (tile_rows[0, 0], tile_cols[0, 0], tile_counts[0, 0], early[0])
        row_ids, col_ids, count, _ = lax.optimization_barrier(given)
        offset = ((row_ids >> 1) - z) & (GZ - 1)
        half = row_ids & 1
        rank = sum(jnp.where(offset == d, PLACE_OF_OFFSET[d], 0) for d in range(GZ))
        sources = source_slots(col_ids)
        forward = group_tiles(rank * 2 + half, sources, 64, count, 16, FWD, FWD_GROUPS, EARLY)
        slots, late = gradient_slots(offset, half)
        reverse = group_tiles(late * 64 + sources, slots, 16, count, 128, BWD, BWD_GROUPS, 64)
        ready = (forward, reverse, labels, place, adj_tiles[0, 0])
        *ready, tiles = lax.optimization_barrier(ready)
        return (*ready, hold_tiles(tiles, early[0]))

    early, late, done = gather_row(features, prepare)
    forward, reverse, labels, place, tiles = done
    parts, _ = spread_and_reduce(
        aggregate_early_kernel,
        aggregate_late_kernel,
        "aggregate",
        forward,
        (tiles, *early, *late),
        (),
        (TB, FEAT),
        (ROWS, FEAT),
    )
    agg, weight_one_t, weight_two_t, weight_two = middle(parts, weight_one, second_t)
    early, late, begun = gather_row(
        agg, functools.partial(early_gates, weight_one_t, weight_two_t)
    )
    parts, panel = spread_and_reduce(
        logits_early_kernel,
        logits_late_kernel,
        "partial_logits",
        forward,
        (tiles, weight_one_t, weight_two_t, begun[0], *late),
        panel_shapes(sum(p.shape[0] for p in late)),
        (CPAD, TB),
        (CPAD, ROWS),
    )
    logits_t, grad_t = loss_grad(parts, labels, place, node_total ** (-0.5))
    near, up, down = gather_col(grad_t)
    total = backward_early(reverse, tiles, near)
    grads = backward_late(
        reverse, tiles, weight_two, total, (*begun[1:], *panel), up, down
    )
    grad_one, grad_two_t = unpack(sum_everywhere(grads))
    return logits_t.T, grad_one, grad_two_t.T


def solution(mesh):
    in_specs = (
        P(("row", "col"), None),
        P(),
        P(),
        P("row", "col", None, None, None),
        P("row", "col", None),
        P("row", "col", None),
        P("row", "col"),
        P("row"),
    )
    out_specs = (P(("row", "col"), None), P(), P())
    return jax.shard_map(body, mesh=mesh, in_specs=in_specs, out_specs=out_specs, check_vma=False)
```

```python
import functools

import jax
import jax.numpy as jnp
from jax import lax
from jax.experimental import pallas as pl
from jax.experimental.pallas import tpu as pltpu
from jax.sharding import PartitionSpec as P

F32 = jnp.float32
BF16 = jnp.bfloat16
NT = (((1,), (1,)), ((), ()))
NN = (((1,), (0,)), ((), ()))
TB = 128
GX, GY, GZ = 4, 4, 8
ROWS = 256
FEAT = 256
CLASSES = 172
CPAD = 176
SLOTS = 128
FWD = 4
BWD = 2
UNROLL = 4
FWD_GROUPS = 52
BWD_GROUPS = 136
CHUNK = 1024
EARLY = 6
PLACE_OF_OFFSET = (7, 3, 4, 0, 1, 2, 5, 6)


def params(mib):
    return pltpu.CompilerParams(vmem_limit_bytes=mib * 1024 * 1024)


def vmem_spec():
    return pl.BlockSpec(memory_space=pltpu.VMEM)


def hbm_spec():
    return pl.BlockSpec(memory_space=pltpu.HBM)


def smem_spec():
    return pl.BlockSpec(memory_space=pltpu.SMEM)


def hold_kernel(tiles_hbm, after, tiles, sem):
    copy = pltpu.make_async_copy(tiles_hbm, tiles, sem)
    copy.start()
    copy.wait()


def hold_tiles(tiles, after):
    return pl.pallas_call(
        hold_kernel,
        name="hold_tiles",
        out_shape=jax.ShapeDtypeStruct(tiles.shape, tiles.dtype),
        in_specs=[hbm_spec(), vmem_spec()],
        out_specs=vmem_spec(),
        scratch_shapes=[pltpu.SemaphoreType.DMA],
        compiler_params=params(4),
        cost_estimate=pl.CostEstimate(flops=0, bytes_accessed=10**3, transcendentals=0),
    )(tiles, after)


def row_perm(move):
    pairs = []
    for index in range(GX * GY * 2):
        x, y, core = index // (2 * GY), (index // 2) % GY, index % 2
        x, y, core = move(x, y, core)
        pairs.append((index, ((x % GX) * GY + y % GY) * 2 + core))
    return pairs


def first_axis(step):
    return row_perm(lambda x, y, c: (x, y + step, c) if c == 0 else (x + step, y, c))


def second_axis(step):
    return row_perm(lambda x, y, c: (x + step, y, c) if c == 0 else (x, y + step, c))


def swap_core():
    return row_perm(lambda x, y, c: (x, y, 1 - c))


def gather_row(own, beside):
    send = lambda v, perm: lax.ppermute(v, "row", perm)
    line = jnp.concatenate(
        [
            own,
            send(own, first_axis(-1)),
            send(own, first_axis(2)),
            send(own, first_axis(1)),
        ],
        0,
    )
    plus = send(line, second_axis(-1))
    minus = send(line, second_axis(1))
    two = send(line, second_axis(2))
    line, plus = lax.optimization_barrier((line, plus))
    early = [line, plus, minus]
    swapped = [send(v, swap_core()) for v in early]
    two, done = lax.optimization_barrier((two, beside(early)))
    return early, swapped, [two, send(two, swap_core())], done


def source_slots(col_ids):
    me = lax.axis_index("row")
    device = col_ids >> 1
    dx = ((device >> 3) - (me >> 3)) & (GX - 1)
    dy = ((device >> 1) - (me >> 1)) & (GY - 1)
    other = device & 1
    along_first = jnp.where(other == 0, dy, dx)
    along_second = jnp.where(other == 0, dx, dy)
    swapped = (other ^ me) & 1
    line = swapped * 3 + jnp.where(along_second == 3, 2, along_second)
    line = jnp.where(along_second == 2, 6 + swapped, line)
    return (line * 4 + along_first) * 2 + (col_ids & 1)


def along_col(value, step):
    return lax.ppermute(value, "col", [(i, (i + step) % GZ) for i in range(GZ)])


def gather_col(own):
    near = {d: along_col(own, -d if d < 4 else GZ - d) for d in (2, 6, 1, 7)}
    up = jnp.concatenate([near[1], near[2][:, :TB]], 1)
    down = jnp.concatenate([near[6][:, TB:], near[7]], 1)
    up, down = along_col(up, -2), along_col(down, 2)
    return [own] + [near[d] for d in (1, 2, 6, 7)], up, down


def gradient_slots(offset, half):
    early = jnp.where(offset > 5, offset - 3, offset) * 2 + half
    late = offset * 2 + half + 4
    is_late = (offset >= 3) & (offset <= 5)
    return jnp.where(is_late, late, early), is_late.astype(jnp.int32)


def reduce_col(up, down, late):
    up, down = along_col(up, 2), along_col(down, -2)
    one, two, six, seven = late()
    width = one.shape[1]
    half = jnp.zeros((one.shape[0], width // 2), F32)
    extra_up = jnp.concatenate([up[:, width:].astype(F32), half], 1)
    extra_down = jnp.concatenate([half, down[:, width:].astype(F32)], 1)
    return [
        along_col((two + extra_up).astype(BF16), 2),
        along_col((six + extra_down).astype(BF16), -2),
        along_col((one + up[:, :width].astype(F32)).astype(BF16), 1),
        along_col((seven + down[:, :width].astype(F32)).astype(BF16), -1),
    ]


def group_tiles(target, source, empty, count, n_targets, group, n_groups, early):
    slots = jnp.arange(SLOTS, dtype=jnp.int32)
    live = slots < count
    key = jnp.where(live, target, n_targets)
    targets = jnp.arange(n_targets, dtype=jnp.int32)
    members = jnp.sum((key[None, :] == targets[:, None]).astype(jnp.int32), 1)
    groups = (members + group - 1) >> (group.bit_length() - 1)
    n_early = jnp.sum(jnp.where(targets < early, groups, 0))
    n_early = (n_early + UNROLL - 1) & -UNROLL
    n_all = n_early + jnp.sum(jnp.where(targets >= early, groups, 0))
    before = (targets[None, :] < key[:, None]) & (
        (targets[None, :] >= early) == (key[:, None] >= early)
    )
    earlier = jnp.sum(jnp.where(before, groups[None, :], 0), 1)
    earlier = earlier + jnp.where(key >= early, n_early, 0)
    rank = jnp.sum(
        ((key[None, :] == key[:, None]) & (slots[None, :] < slots[:, None])).astype(jnp.int32), 1
    )
    place = jnp.where(live, earlier * group + rank, -1)
    places = jnp.arange(n_groups * group, dtype=jnp.int32)
    hit = place[None, :] == places[:, None]
    order = jnp.sum(jnp.where(hit, slots[None, :], 0), 1)
    picked = empty + jnp.sum(jnp.where(hit, source[None, :] - empty, 0), 1)
    first = place[None, :] == group * jnp.arange(n_groups, dtype=jnp.int32)[:, None]
    goal = jnp.sum(jnp.where(first, target[None, :], 0), 1)
    counts = jnp.where(jnp.arange(2) == 0, n_early, n_all)
    return order, picked, goal, counts


def run_groups(table, group, first, last, shift, product, total):
    order, picked, goal, _ = table

    def step(i, carry):
        made = []
        for u in range(UNROLL):
            start = (i * UNROLL + u) * group
            tiles = [order[start + k] for k in range(group)]
            sources = [picked[start + k] for k in range(group)]
            made.append(product(tiles, sources))
        for u in range(UNROLL):
            total[jnp.maximum(goal[i * UNROLL + u] - shift, 0)] += made[u]
        return carry

    lax.fori_loop(first // UNROLL, (last + UNROLL - 1) // UNROLL, step, 0)


def clear(ref):
    def step(i, carry):
        ref[i] = jnp.zeros(ref.shape[1:], ref.dtype)
        return carry

    lax.fori_loop(0, ref.shape[0], step, 0)


def copy_rows(piece, panel, start, rows):
    def step(i, carry):
        origin = pl.ds(pl.multiple_of(i * rows, rows), rows)
        target = pl.ds(pl.multiple_of(start + i * rows, rows), rows)
        panel[target, :] = piece[origin, :]
        return carry

    lax.fori_loop(0, piece.shape[0] // rows, step, 0)


def rows_product(tiles, source):
    def product(picked, origins):
        return lax.dot_general(
            jnp.concatenate([tiles[t] for t in picked], 1),
            jnp.concatenate([source[o] for o in origins], 0),
            NN,
            preferred_element_type=F32,
        )

    return product


def columns_product(tiles, source):
    def product(picked, origins):
        return lax.dot_general(
            jnp.concatenate([source[o] for o in origins], 1),
            jnp.concatenate([tiles[t] for t in picked], 1),
            NT,
            preferred_element_type=F32,
        )

    return product


def halves_of_rows(total, place):
    return jnp.concatenate([total[2 * place], total[2 * place + 1]], 0)


def halves_of_columns(total, place):
    return jnp.concatenate([total[2 * place], total[2 * place + 1]], 1)


def early_outputs(total, whole, out_up, out_down):
    far = whole(total, 1)
    width = far.shape[1]
    out_up[:, :width] = whole(total, 0).astype(BF16)
    out_up[:, width:] = far[:, : width // 2].astype(BF16)
    out_down[:, :width] = whole(total, 2).astype(BF16)
    out_down[:, width:] = far[:, width // 2 :].astype(BF16)


def aggregate_early_kernel(*refs):
    table, (tiles, *rest) = refs[:4], refs[4:]
    pieces, (source, out_up, out_down, total) = rest[:-4], rest[-4:]
    filled = 0
    for piece in pieces:

        def step(i, carry):
            source[filled + i] = piece[pl.ds(pl.multiple_of(i * TB, TB), TB), :]
            return carry

        lax.fori_loop(0, piece.shape[0] // TB, step, 0)
        filled += piece.shape[0] // TB
    source[filled] = jnp.zeros((TB, FEAT), BF16)
    clear(total)
    run_groups(table, FWD, 0, table[3][0], 0, rows_product(tiles, source), total)
    early_outputs(total, halves_of_rows, out_up, out_down)


def aggregate_late_kernel(*refs):
    table, (tiles, source, *rest) = refs[:4], refs[4:]
    outs, total = rest[:5], rest[5]
    clear(total)
    run_groups(table, FWD, table[3][0], table[3][1], EARLY, rows_product(tiles, source), total)
    for place, out in enumerate(outs):
        out[...] = halves_of_rows(total, place)


def sigmoid(value):
    return 0.5 * jnp.tanh(0.5 * value) + 0.5


def gates(pieces, weight_one_t, weight_two_t, source, agg, hidden_t, slope_t):
    filled = 0
    for piece in pieces:
        copy_rows(piece, agg, filled, ROWS)
        filled += piece.shape[0]

    def step(i, carry):
        span = pl.ds(pl.multiple_of(i * CHUNK, CHUNK), CHUNK)
        pre = lax.dot_general(weight_one_t[...], agg[span, :], NT, preferred_element_type=F32)
        gate = sigmoid(pre)
        hidden = (pre * gate).astype(BF16)
        hidden_t[:, span] = hidden
        slope_t[:, span] = (gate * (1.0 + pre * (1.0 - gate))).astype(BF16)
        projected = lax.dot_general(
            weight_two_t[...], hidden, NN, preferred_element_type=F32
        ).astype(BF16)
        for block in range(CHUNK // TB):
            source[i * (CHUNK // TB) + block] = projected[:, block * TB : (block + 1) * TB]
        return carry

    lax.fori_loop(0, filled // CHUNK, step, 0)


def panel_shapes(nodes):
    return (
        jax.ShapeDtypeStruct((nodes, FEAT), BF16),
        jax.ShapeDtypeStruct((FEAT, nodes), BF16),
        jax.ShapeDtypeStruct((FEAT, nodes), BF16),
    )


def gates_kernel(weight_one_t, weight_two_t, *rest):
    gates(rest[:-4], weight_one_t, weight_two_t, *rest[-4:])


def early_gates(weight_one_t, weight_two_t, pieces):
    nodes = sum(p.shape[0] for p in pieces)
    return pl.pallas_call(
        gates_kernel,
        name="early_gates",
        out_shape=(
            jax.ShapeDtypeStruct((nodes // TB, CPAD, TB), BF16),
            *panel_shapes(nodes),
        ),
        in_specs=[vmem_spec()] * (2 + len(pieces)),
        out_specs=[vmem_spec()] * 4,
        compiler_params=params(8),
        cost_estimate=pl.CostEstimate(flops=10**3, bytes_accessed=10**3, transcendentals=0),
    )(weight_one_t, weight_two_t, *pieces)


def logits_early_kernel(*refs):
    table, (tiles, weight_one_t, weight_two_t, *rest) = refs[:4], refs[4:]
    begun, rest = rest[:2], rest[2:]
    pieces, rest = rest[:-7], rest[-7:]
    source, out_up, out_down, agg, hidden_t, slope_t, total = rest
    blocks = 0
    for part in begun:

        def step(i, carry):
            source[blocks + i] = part[i]
            return carry

        lax.fori_loop(0, part.shape[0], step, 0)
        blocks += part.shape[0]
    later = source.at[pl.ds(blocks, 64 - blocks)]
    gates(pieces, weight_one_t, weight_two_t, later, agg, hidden_t, slope_t)
    source[64] = jnp.zeros((CPAD, TB), BF16)
    clear(total)
    run_groups(table, FWD, 0, table[3][0], 0, columns_product(tiles, source), total)
    early_outputs(total, halves_of_columns, out_up, out_down)


def logits_late_kernel(*refs):
    table, (tiles, source, *rest) = refs[:4], refs[4:]
    outs, total = rest[:5], rest[5]
    clear(total)
    run_groups(table, FWD, table[3][0], table[3][1], EARLY, columns_product(tiles, source), total)
    for place, out in enumerate(outs):
        out[...] = halves_of_columns(total, place)


def spread_and_reduce(early_kernel, late_kernel, name, table, operands, kept, block, out):
    cost = pl.CostEstimate(flops=10**9, bytes_accessed=10**7, transcendentals=0)
    wide = jax.ShapeDtypeStruct((out[0], out[1] * 3 // 2), BF16)
    source, up, down, *kept = pl.pallas_call(
        early_kernel,
        name=name + "_early",
        out_shape=(jax.ShapeDtypeStruct((65, *block), BF16), wide, wide, *kept),
        in_specs=[smem_spec()] * 4 + [vmem_spec()] * len(operands),
        out_specs=[vmem_spec()] * (3 + len(kept)),
        scratch_shapes=[pltpu.VMEM((EARLY, *block), F32)],
        compiler_params=params(10),
        cost_estimate=cost,
    )(*table, *operands)
    *late, own = pl.pallas_call(
        late_kernel,
        name=name + "_late",
        out_shape=(jax.ShapeDtypeStruct(out, F32),) * 5,
        in_specs=[smem_spec()] * 4 + [vmem_spec()] * 2,
        out_specs=[vmem_spec()] * 5,
        scratch_shapes=[pltpu.VMEM((16 - EARLY, *block), F32)],
        compiler_params=params(8),
        cost_estimate=cost,
    )(*table, operands[0], source)
    return [own] + reduce_col(up, down, lambda: late), kept


def add_up(parts):
    summed = parts[0][...].astype(F32)
    for part in parts[1:]:
        summed += part[...].astype(F32)
    return summed


def middle_kernel(*refs):
    parts, (one, two_t, agg, one_t, wide_t, wide, padded) = refs[:5], refs[5:]
    agg[...] = add_up(parts).astype(BF16)
    one_t[...] = jnp.transpose(one[...].astype(F32)).astype(BF16)
    padded[...] = jnp.zeros_like(padded)
    padded[0:CLASSES] = two_t[...].astype(F32)
    wide_t[...] = padded[...].astype(BF16)
    wide[...] = jnp.transpose(padded[...]).astype(BF16)


def middle(parts, weight_one, weight_two_t):
    return pl.pallas_call(
        middle_kernel,
        name="middle",
        out_shape=(
            jax.ShapeDtypeStruct((ROWS, FEAT), BF16),
            jax.ShapeDtypeStruct((FEAT, FEAT), BF16),
            jax.ShapeDtypeStruct((CPAD, FEAT), BF16),
            jax.ShapeDtypeStruct((FEAT, CPAD), BF16),
        ),
        in_specs=[vmem_spec()] * 7,
        out_specs=[vmem_spec()] * 4,
        scratch_shapes=[pltpu.VMEM((CPAD, FEAT), F32)],
        compiler_params=params(8),
    )(*parts, weight_one, weight_two_t)


def loss_kernel(scale, *refs):
    parts, (labels, place, logits_t, grad_t) = refs[:5], refs[5:]
    summed = add_up(parts)
    logits_t[...] = summed[:CLASSES]
    ids = lax.broadcasted_iota(jnp.int32, summed.shape, 0)
    valid = ids < CLASSES
    top = jnp.max(jnp.where(valid, summed, -jnp.inf), 0, keepdims=True)
    grown = jnp.where(valid, jnp.exp(summed - top), 0.0)
    soft = grown / jnp.sum(grown, 0, keepdims=True)
    own_labels = jnp.concatenate([labels[pl.ds(place[0] * 2 + k, 1), :] for k in range(2)], 1)
    onehot = (ids == own_labels).astype(F32)
    grad_t[...] = ((soft - onehot) * scale).astype(BF16)


def loss_grad(parts, labels, place, scale):
    return pl.pallas_call(
        functools.partial(loss_kernel, scale),
        name="loss_grad",
        out_shape=(
            jax.ShapeDtypeStruct((CLASSES, ROWS), F32),
            jax.ShapeDtypeStruct((CPAD, ROWS), BF16),
        ),
        in_specs=[vmem_spec()] * 6 + [smem_spec()],
        out_specs=[vmem_spec()] * 2,
        compiler_params=params(8),
    )(*parts, labels, place)


def backward_tiles(table, first, last, shift, tiles, grads, total):
    def product(picked, origins):
        return lax.dot_general(
            jnp.concatenate([grads[o] for o in origins], 1),
            jnp.concatenate([tiles[t] for t in picked], 0),
            NN,
            preferred_element_type=F32,
        )

    run_groups(table, BWD, first, last, shift, product, total)


def backward_early_kernel(*refs):
    table, (tiles, *pieces), (total, grads) = refs[:4], refs[4:-2], refs[-2:]
    for place, piece in enumerate(pieces):
        grads[2 * place] = piece[:, :TB]
        grads[2 * place + 1] = piece[:, TB:]
    grads[16] = jnp.zeros((CPAD, TB), BF16)
    clear(total)
    backward_tiles(table, 0, table[3][0], 0, tiles, grads, total)


def backward_early(table, tiles, pieces):
    return pl.pallas_call(
        backward_early_kernel,
        name="backward_early",
        out_shape=jax.ShapeDtypeStruct((64, CPAD, TB), F32),
        in_specs=[smem_spec()] * 4 + [vmem_spec()] * (1 + len(pieces)),
        out_specs=vmem_spec(),
        scratch_shapes=[pltpu.VMEM((17, CPAD, TB), BF16)],
        compiler_params=params(8),
        cost_estimate=pl.CostEstimate(flops=10**3, bytes_accessed=10**3, transcendentals=0),
    )(*table, tiles, *pieces)


def backward_late_kernel(*refs):
    table, (tiles, weight_two, begun, *rest) = refs[:4], refs[4:]
    panels, (up, down, *rest) = (rest[0:3], rest[3:6], rest[6:9]), rest[9:]
    out, grads, total, sum_one, sum_two = rest
    for place, piece in enumerate((up, down)):
        for k in range(3):
            grads[10 + 3 * place + k] = piece[:, k * TB : (k + 1) * TB]
    grads[16] = jnp.zeros((CPAD, TB), BF16)

    def take(i, carry):
        total[i] = begun[i]
        return carry

    lax.fori_loop(0, 64, take, 0)
    backward_tiles(table, table[3][0], table[3][1], 64, tiles, grads, total)
    sum_one[...] = jnp.zeros_like(sum_one)
    sum_two[...] = jnp.zeros_like(sum_two)
    blocks = 8
    span = blocks * TB
    done = 0
    for agg, hidden, slope in panels:

        def finish(i, carry):
            held = [total[done + i * blocks + k] for k in range(blocks)]
            back = jnp.concatenate(held, 1).astype(BF16)
            part = pl.ds(pl.multiple_of(i * span, span), span)
            grad = lax.dot_general(weight_two[...], back, NN, preferred_element_type=F32)
            grad = (grad * slope[:, part].astype(F32)).astype(BF16)
            sum_one[...] += lax.dot_general(grad, agg[part, :], NN, preferred_element_type=F32)
            sum_two[...] += lax.dot_general(back, hidden[:, part], NT, preferred_element_type=F32)
            return carry

        lax.fori_loop(0, agg.shape[0] // span, finish, 0)
        done += agg.shape[0] // TB
    out[0:FEAT] = jnp.transpose(sum_one[...]).astype(BF16)
    out[FEAT : FEAT + CPAD] = sum_two[...].astype(BF16)
    out[FEAT + CPAD :] = jnp.zeros((512 - FEAT - CPAD, FEAT), BF16)


def backward_late(table, tiles, weight_two, begun, panels, up, down):
    return pl.pallas_call(
        backward_late_kernel,
        name="backward_late",
        out_shape=jax.ShapeDtypeStruct((512, FEAT), BF16),
        in_specs=[smem_spec()] * 4 + [vmem_spec()] * (5 + len(panels)),
        out_specs=vmem_spec(),
        scratch_shapes=[
            pltpu.VMEM((17, CPAD, TB), BF16),
            pltpu.VMEM((64, CPAD, TB), F32),
            pltpu.VMEM((FEAT, FEAT), F32),
            pltpu.VMEM((CPAD, FEAT), F32),
        ],
        compiler_params=params(12),
        cost_estimate=pl.CostEstimate(flops=5 * 10**9, bytes_accessed=2 * 10**7, transcendentals=0),
    )(*table, tiles, weight_two, begun, *panels, up, down)


def sum_everywhere(grads):
    shares = lax.all_to_all(grads.reshape(32, 16, FEAT), "row", 0, 0, tiled=True)
    share = jnp.sum(shares.astype(F32), 0).astype(BF16)
    shares = lax.all_to_all(
        jnp.broadcast_to(share, (GZ, 16, FEAT)), "col", 0, 0, tiled=True
    )
    share = jnp.sum(shares.astype(F32), 0).astype(BF16)
    full = lax.all_to_all(jnp.broadcast_to(share, (32, 16, FEAT)), "row", 0, 0, tiled=True)
    return full.reshape(512, FEAT)


def unpack_kernel(grads, grad_one, grad_two_t):
    grad_one[...] = grads[0:FEAT].astype(F32)
    grad_two_t[...] = grads[FEAT : FEAT + CPAD].astype(F32)[:CLASSES]


def unpack(grads):
    return pl.pallas_call(
        unpack_kernel,
        name="unpack",
        out_shape=(
            jax.ShapeDtypeStruct((FEAT, FEAT), F32),
            jax.ShapeDtypeStruct((CLASSES, FEAT), F32),
        ),
        in_specs=[vmem_spec()],
        out_specs=[vmem_spec()] * 2,
        compiler_params=params(4),
    )(grads)


def body(features, weight_one, weight_two, adj_tiles, tile_rows, tile_cols, tile_counts, labels):
    z = lax.axis_index("col")
    node_total = ROWS * lax.axis_size("row") * lax.axis_size("col")
    labels = labels.reshape(GZ * ROWS // TB, TB)
    place = jnp.full((1,), z, jnp.int32)
    second_t = weight_two.T

    def prepare(early):
        given = (tile_rows[0, 0], tile_cols[0, 0], tile_counts[0, 0], early[0])
        row_ids, col_ids, count, _ = lax.optimization_barrier(given)
        offset = ((row_ids >> 1) - z) & (GZ - 1)
        half = row_ids & 1
        rank = sum(jnp.where(offset == d, PLACE_OF_OFFSET[d], 0) for d in range(GZ))
        sources = source_slots(col_ids)
        forward = group_tiles(rank * 2 + half, sources, 64, count, 16, FWD, FWD_GROUPS, EARLY)
        slots, late = gradient_slots(offset, half)
        reverse = group_tiles(late * 64 + sources, slots, 16, count, 128, BWD, BWD_GROUPS, 64)
        ready = (forward, reverse, labels, place, adj_tiles[0, 0])
        *ready, tiles = lax.optimization_barrier(ready)
        return (*ready, hold_tiles(tiles, early[0]))

    *pieces, done = gather_row(features, prepare)
    forward, reverse, labels, place, tiles = done
    parts, _ = spread_and_reduce(
        aggregate_early_kernel,
        aggregate_late_kernel,
        "aggregate",
        forward,
        (tiles, *pieces[0], *pieces[1], *pieces[2]),
        (),
        (TB, FEAT),
        (ROWS, FEAT),
    )
    agg, weight_one_t, weight_two_t, weight_two = middle(parts, weight_one, second_t)
    _, swapped, late, begun = gather_row(
        agg, functools.partial(early_gates, weight_one_t, weight_two_t)
    )
    more = early_gates(weight_one_t, weight_two_t, swapped)
    parts, panel = spread_and_reduce(
        logits_early_kernel,
        logits_late_kernel,
        "partial_logits",
        forward,
        (tiles, weight_one_t, weight_two_t, begun[0], more[0], *late),
        panel_shapes(sum(p.shape[0] for p in late)),
        (CPAD, TB),
        (CPAD, ROWS),
    )
    logits_t, grad_t = loss_grad(parts, labels, place, node_total ** (-0.5))
    near, up, down = gather_col(grad_t)
    total = backward_early(reverse, tiles, near)
    grads = backward_late(
        reverse, tiles, weight_two, total, (*begun[1:], *more[1:], *panel), up, down
    )
    grad_one, grad_two_t = unpack(sum_everywhere(grads))
    return logits_t.T, grad_one, grad_two_t.T


def solution(mesh):
    in_specs = (
        P(("row", "col"), None),
        P(),
        P(),
        P("row", "col", None, None, None),
        P("row", "col", None),
        P("row", "col", None),
        P("row", "col"),
        P("row"),
    )
    out_specs = (P(("row", "col"), None), P(), P())
    return jax.shard_map(body, mesh=mesh, in_specs=in_specs, out_specs=out_specs, check_vma=False)
```
